32 devices in a mesh: sets: 4 (over y, core), pts: 8 (over z, x).
Axes of the slice: x: 2, y: 2, z: 4, core: 2. Of those that a mesh axis runs over, the one named last changes fastest.
Arguments:
- points: bfloat16 [65536, 128], P(('sets', 'pts')), may hold values from -6 to 6
- set_lengths: int32 [124], P('sets'), may hold values from 64 to 512, as said below
- projections: bfloat16 [3, 3, 128, 128], replicated, may hold values from -0.75 to 0.75
- outputs: bfloat16 [3, 128, 128], replicated, may hold values from -1.5 to 1.5
- feedforward: bfloat16 [3, 2, 128, 128], replicated, may hold values from -0.5 to 0.5
- gains: bfloat16 [3, 2, 128], replicated, may hold values from 0.25 to 1.75
- inducing: bfloat16 [32, 128], replicated, may hold values from -6 to 6
- seeds: bfloat16 [4, 128], replicated, may hold values from -6 to 6
- cotangent: bfloat16 [124, 4, 128], P('sets'), may hold values from -6 to 6
Outputs:
- pooled: bfloat16 [124, 4, 128], P('sets')
- points_grad: bfloat16 [65536, 128], P(('sets', 'pts'))
- projections_grad: float32 [3, 3, 128, 128], replicated
- outputs_grad: float32 [3, 128, 128], replicated
- feedforward_grad: float32 [3, 2, 128, 128], replicated
- gains_grad: float32 [3, 2, 128], replicated
- inducing_grad: float32 [32, 128], replicated
- seeds_grad: float32 [4, 128], replicated
The draws below stay inside these ranges and needn't reach their ends.
Inputs may be any that keep to these rules, and one draw needn't show every extreme that they name: `set_lengths`: in every group of 31 consecutive sets one set has exactly 512 points and one exactly 64.
All inputs are finite; a program needn't handle non-finite values.
Results may differ from the reference program's by a relative error of at most 0.04.
The reference program's roundings to bfloat16 on the way count: a program that leaves them out, or rounds other values in their place, can miss the bound.
Values may be sent and summed in bfloat16 or wider, within the bound.
A program may use at most 384 MiB of HBM per device.

```python
import jax
import jax.numpy as jnp
from jax import lax

D = 128
HEADS = 4
HEAD_DIM = 32
FF = 128
INDUCING = 32
SEEDS = 4
TOK_DEV = 2048
LEN_MAX = 512
LEN_MIN = 64
SEGS = 31
ALL_SETS = 124
TOKENS = 65536
N_PTS = 8


def draw_set_lengths(key, part):
    key = jax.random.fold_in(key, 11)
    first_key, second_key = jax.random.split(key, 2)
    groups = ALL_SETS // SEGS
    lengths = jax.random.randint(first_key, (groups, SEGS), LEN_MIN, LEN_MAX + 1)
    lengths = lengths.at[:, 0].set(LEN_MAX).at[:, 1].set(LEN_MIN)
    turned = jax.random.randint(second_key, (groups, 1), 0, SEGS)
    order = (jnp.arange(SEGS, dtype=jnp.int32)[None, :] + turned) % SEGS
    return jnp.take_along_axis(lengths, order, axis=1).reshape(ALL_SETS).astype(jnp.int32)


def levels(key, shape, cuts, low, largest):
    factor_of = 1.0
    for axis_at, parts in cuts:
        heights = jax.random.uniform(jax.random.fold_in(jax.random.fold_in(key, 6), axis_at), (parts,), jnp.float32, low / len(cuts), largest / len(cuts))
        factor_of = factor_of * jnp.repeat(jnp.exp(heights), shape[axis_at] // parts).reshape((-1,) + (1,) * (len(shape) - 1 - axis_at))
    return factor_of


def gaussian(own_key, dims, scale, reach, cuts=(), kind=jnp.bfloat16):
    level = levels(own_key, dims, cuts, -0.22, 0.18) if cuts else 1.0
    array = jax.random.normal(own_key, dims, jnp.float32) * scale * level
    return jnp.minimum(jnp.maximum(array, -reach), reach).astype(kind)


def setup_inputs(seed: int = 0) -> dict:
    key_of = jax.random.split(jax.random.key(seed), 10)
    points = gaussian(key_of[0], (TOKENS, D), 1.0, 6.0, ((0, 32),))
    set_lengths = draw_set_lengths(jax.random.fold_in(key_of[9], 71), 0)
    projections = gaussian(key_of[2], (3, 3, D, D), (D // 2) ** -0.5, 0.75)
    outputs = gaussian(key_of[3], (3, D, D), (D // 8) ** -0.5, 1.5)
    feedforward = gaussian(key_of[4], (3, 2, D, FF), D ** -0.5, 0.5)
    gains = jnp.clip(1.0 + 0.15 * jax.random.normal(key_of[5], (3, 2, D), jnp.float32), 0.25, 1.75).astype(jnp.bfloat16)
    inducing = gaussian(key_of[6], (INDUCING, D), 1.0, 6.0)
    seeds = gaussian(key_of[7], (SEEDS, D), 1.0, 6.0)
    cotangent = gaussian(key_of[8], (ALL_SETS, SEEDS, D), 1.0, 6.0, ((0, 4),))
    return dict(points=points, set_lengths=set_lengths, projections=projections, outputs=outputs, feedforward=feedforward, gains=gains, inducing=inducing, seeds=seeds, cotangent=cotangent)


@jax.custom_vjp
def low(v):
    return lax.optimization_barrier(v.astype(jnp.bfloat16)).astype(jnp.float32)

@jax.custom_vjp
def low_back(v):
    return v

def low_keep(v):
    return (low(v), None)

def low_pass(kept, grad):
    return (grad,)

def back_keep(v):
    return (v, None)

def back_low(kept, grad):
    return (low(grad),)
low.defvjp(low_keep, low_pass)
low_back.defvjp(back_keep, back_low)
HIGHEST = lax.Precision.HIGHEST
NEG_FILL = -1e+30

def matmul(operand, weight_mat):
    return jnp.dot(operand, weight_mat, precision=HIGHEST, preferred_element_type=jnp.float32)

def layer_norm(values, gain):
    center = values - lax.optimization_barrier(jnp.mean(values, axis=-1, keepdims=True))
    spread = lax.optimization_barrier(jnp.mean(center * center, axis=-1, keepdims=True))
    return gain * center * lax.rsqrt(spread + 1e-05)

def membership(lengths):
    device = jnp.arange(N_PTS, dtype=jnp.int32)
    counts = (lengths[:, None] - device[None, :] + N_PTS - 1) // N_PTS
    finish = jnp.cumsum(counts, axis=0)
    starts = finish - counts
    slot_ids = jnp.arange(TOK_DEV, dtype=jnp.int32)
    inside = (slot_ids[None, None, :] >= starts[:, :, None]) & (slot_ids[None, None, :] < finish[:, :, None])
    return inside.astype(jnp.float32).transpose(1, 2, 0).reshape(N_PTS * TOK_DEV, SEGS)

def tail(query, attended, out_weight, up_weight, down_weight, gain_first, gain_second):
    mixed_rows = low_back(matmul(low(attended), out_weight))
    normed = layer_norm(query + mixed_rows, gain_first)
    inner_pre = low_back(matmul(low(normed), up_weight))
    branch = low_back(matmul(low(jax.nn.gelu(inner_pre)), down_weight))
    return layer_norm(normed + branch, gain_second)

def pooled_attention(queries, keys, values, member):
    row_count = queries.shape[0]
    query_grid = queries.reshape(row_count, HEADS, HEAD_DIM)
    key_grid = keys.reshape(-1, HEADS, HEAD_DIM)
    value_grid = values.reshape(-1, HEADS, HEAD_DIM)
    scores = low_back(jnp.einsum('nhc,rhc->nhr', key_grid, query_grid, precision=HIGHEST))
    inside = member.T[:, :, None, None] > 0
    highest = lax.optimization_barrier(jnp.max(jnp.where(inside, scores[None], NEG_FILL), axis=1))
    shifted = jnp.einsum('ng,ghr->nhr', member, highest, precision=HIGHEST)
    filled = lax.optimization_barrier(jnp.sum(member, axis=1))[:, None, None] > 0
    weights = jnp.where(filled, jnp.exp(scores - shifted), 0.0)
    totals = jnp.einsum('ng,nhr->ghr', member, weights, precision=HIGHEST)
    numerator = low_back(jnp.einsum('ng,nhr,nhc->grhc', member, low(weights), value_grid, precision=HIGHEST))
    return (numerator / totals.transpose(0, 2, 1)[:, :, :, None]).reshape(-1, row_count, D)

def point_attention(queries, keys, values, allowed):
    query_grid = queries.reshape(-1, HEADS, HEAD_DIM)
    key_grid = keys.reshape(-1, HEADS, HEAD_DIM)
    value_grid = values.reshape(-1, HEADS, HEAD_DIM)
    scores = low_back(jnp.einsum('nhc,khc->nhk', query_grid, key_grid, precision=HIGHEST))
    masked = jnp.where(allowed[:, None, :], scores, NEG_FILL)
    highest = lax.optimization_barrier(jnp.max(masked, axis=2, keepdims=True))
    weights = jnp.where(allowed[:, None, :], jnp.exp(masked - highest), 0.0)
    totals = lax.optimization_barrier(jnp.sum(weights, axis=2))
    numerator = low_back(jnp.einsum('nhk,khc->nhc', low(weights), value_grid, precision=HIGHEST))
    return (numerator / totals[:, :, None]).reshape(-1, D)

def group_forward(group_points, member, projections, outputs, feedforward, gains, inducing, seeds):
    factor = HEAD_DIM ** (-0.5)
    query_one = low(matmul(inducing, projections[0, 0]) * factor)
    key_one = low_back(low(matmul(group_points, projections[0, 1])))
    value_one = low_back(low(matmul(group_points, projections[0, 2])))
    attended_one = pooled_attention(query_one, key_one, value_one, member).reshape(SEGS * INDUCING, D)
    induced = tail(jnp.tile(inducing, (SEGS, 1)), attended_one, outputs[0], feedforward[0, 0], feedforward[0, 1], gains[0, 0], gains[0, 1])
    induced_low = low(induced)
    nearest = member.at[:, 0].add(1.0 - lax.optimization_barrier(jnp.sum(member, axis=1)))
    allowed = jnp.repeat(nearest, INDUCING, axis=1) > 0
    query_two = low(low_back(matmul(group_points, projections[1, 0])) * factor)
    key_two = low_back(low(matmul(induced_low, projections[1, 1])))
    value_two = low_back(low(matmul(induced_low, projections[1, 2])))
    attended_two = point_attention(query_two, key_two, value_two, allowed)
    mixed_rows = tail(group_points, attended_two, outputs[1], feedforward[1, 0], feedforward[1, 1], gains[1, 0], gains[1, 1])
    mixed_low = low(mixed_rows)
    query_three = low(matmul(seeds, projections[2, 0]) * factor)
    key_three = low_back(low(matmul(mixed_low, projections[2, 1])))
    value_three = low_back(low(matmul(mixed_low, projections[2, 2])))
    attended_three = pooled_attention(query_three, key_three, value_three, member).reshape(SEGS * SEEDS, D)
    final = tail(jnp.tile(seeds, (SEGS, 1)), attended_three, outputs[2], feedforward[2, 0], feedforward[2, 1], gains[2, 0], gains[2, 1])
    return final.reshape(SEGS, SEEDS, D)

def reference(points, set_lengths, projections, outputs, feedforward, gains, inducing, seeds, cotangent):
    groups = ALL_SETS // SEGS
    member = jax.vmap(membership)(set_lengths.reshape(groups, SEGS))
    floats = tuple((array_in.astype(jnp.float32) for array_in in (points, projections, outputs, feedforward, gains, inducing, seeds)))

    def forward(points_f, projections_f, outputs_f, feedforward_f, gains_f, inducing_f, seeds_f):
        blocks = points_f.reshape(groups, N_PTS * TOK_DEV, D)

        def one_group(couple):
            return group_forward(couple[0], couple[1], projections_f, outputs_f, feedforward_f, gains_f, inducing_f, seeds_f)
        pooled = lax.map(jax.checkpoint(one_group), (blocks, member))
        return pooled.reshape(ALL_SETS, SEEDS, D)
    pooled, pullback = jax.vjp(forward, *floats)
    gradients = pullback(cotangent.astype(jnp.float32))
    return (pooled.astype(jnp.bfloat16), gradients[0].astype(jnp.bfloat16), gradients[1], gradients[2], gradients[3], gradients[4], gradients[5], gradients[6])
```

```python
import functools
import math

import jax
import jax.numpy as jnp
from jax import lax
from jax.experimental import pallas as pl
from jax.experimental.pallas import tpu as pltpu
from jax.sharding import PartitionSpec as P

MESH = pl.DeviceIdType.MESH
F32 = jnp.float32
BF16 = jnp.bfloat16
D = 128
HEADS = 4
HD = 32
IND = 32
SEEDS = 4
SP = 8
SLOTS = 32
WIN = 64
CS = 4
CR = CS * WIN
NCH = SLOTS // CS
NEG = -1e30
FACTOR = HD**-0.5
G0 = math.sqrt(2.0 / math.pi)
G1 = 0.044715

RS1N, RS1M, AG1, RS2, AG2, AGP, RS3, AG3N, AG3M, GRS, GAG = 0, 1, 2, 3, 4, 5, 6, 7, 8, 9, 12
PHASES = 15


def nn(a, b):
    return lax.dot_general(a, b, (((1,), (0,)), ((), ())), preferred_element_type=F32)


def nt(a, b):
    return lax.dot_general(a, b, (((1,), (1,)), ((), ())), preferred_element_type=F32)


def tn(a, b):
    return lax.dot_general(a, b, (((0,), (0,)), ((), ())), preferred_element_type=F32)


def split(x):
    high = x.astype(BF16)
    return high, (x - high.astype(F32)).astype(BF16)


def iota(shape, dim):
    return lax.broadcasted_iota(jnp.int32, shape, dim)


def norm(values, axis):
    center = values - jnp.mean(values, axis=axis, keepdims=True)
    scale = lax.rsqrt(jnp.mean(center * center, axis=axis, keepdims=True) + 1e-05)
    return center * scale, scale


def norm_back(d_out, gain, hat, scale, axis):
    scaled = d_out * gain
    first = jnp.mean(scaled, axis=axis, keepdims=True)
    second = jnp.mean(scaled * hat, axis=axis, keepdims=True)
    return scale * (scaled - first - hat * second)


def gelu(v):
    th = jnp.tanh(G0 * (v + G1 * (v * v * v)))
    return 0.5 * v * (1.0 + th)


def gelu_both(v):
    sq = v * v
    th = jnp.tanh(G0 * (v + G1 * (sq * v)))
    half = 0.5 * (1.0 + th)
    return v * half, half + 0.5 * v * (1.0 - th * th) * (G0 * (1.0 + 3.0 * G1 * sq))


def slab_rows(rows, parts):
    unit = 16 * parts
    return (rows + unit - 1) // unit * unit


def kernel(
    cfg,
    len_ref, pts_ref, proj_ref, outw_ref, ff_ref, gain_ref, ind_ref, seed_ref, cot_ref,
    pool_o, pg_o, projg_o, outg_o, ffg_o, gaing_o, indg_o, seedg_o,
    starts, counts,
    pf32, pgpad, xT, v1s, q2T, t1s, m1l, t2s, den2s, attT, xh1s, r1s, ps, xh2s, r2s, m2b, kv3T, t3s, dxT, kv2s,
    bd, ones2, diag, half0, gF, w01kv, w1kv, w10T, w2kvT, w2kv, tailT, qB, q3B, q3BT, gW,
    send1, send1m, recv1, recv1m, k2all, send2, recv2, send2b, recv2b, poolrow, poolall,
    send3, recv3, send3b, recv3b, send3m, recv3m,
    wexp, numtot, rdenx, own0, own0r, ea,
    s1, s1b, s1r, s1m, s1mr, s1g,
    s2, s2b, s2r, s2m, s2mr, s2g,
    s3, s3b, s3r, s3m, s3mr, s3g,
    accg,
    ssem, rsem, gssem, grsem,
):
    parts, groups, set_count, spo = cfg
    me = lax.axis_index("pts")
    mine = lax.axis_index("sets")
    opc = CS // spo
    mychunk = me // opc
    ro = spo * IND
    po = spo * SP

    barrier = pltpu.get_barrier_semaphore()
    for k in range(1, parts):
        pl.semaphore_signal(barrier, inc=1, device_id={"pts": lax.rem(me + k, parts)}, device_id_type=MESH)
    for k in range(1, groups):
        pl.semaphore_signal(barrier, inc=1, device_id={"sets": lax.rem(mine + k, groups)}, device_id_type=MESH)

    def copy(ph, src, dst, dev, slot):
        return pltpu.make_async_remote_copy(
            src_ref=src, dst_ref=dst, send_sem=ssem.at[ph, dev], recv_sem=rsem.at[ph, slot],
            device_id={"pts": dev}, device_id_type=MESH,
        )

    def gcopy(ph, src, dst, dev, slot):
        return pltpu.make_async_remote_copy(
            src_ref=src, dst_ref=dst, send_sem=gssem.at[ph, dev], recv_sem=grsem.at[ph, slot],
            device_id={"sets": dev}, device_id_type=MESH,
        )

    row128 = iota((D, D), 0)
    lane128 = iota((D, D), 1)
    same_head = (row128 // HD) == (lane128 // HD)
    bd[...] = jnp.where(same_head, 1.0, 0.0).astype(BF16)
    bdv = bd[...]
    ones2[0:D, :] = bdv
    ones2[D:, :] = bdv
    diag[...] = jnp.where((iota((IND, D), 1) % HD) == iota((IND, D), 0), 1.0, 0.0)
    half0[...] = jnp.where(lane128 < WIN, 1.0, 0.0).astype(BF16)
    w01kv[:, 0:D] = proj_ref[0, 1]
    w01kv[:, D:] = proj_ref[0, 2]
    w1kv[:, 0:D] = proj_ref[1, 1]
    w1kv[:, D:] = proj_ref[1, 2]
    w2kv[:, 0:D] = proj_ref[2, 1]
    w2kv[:, D:] = proj_ref[2, 2]
    w10T[...] = proj_ref[1, 0].T
    w2kvT[0:D, :] = proj_ref[2, 1].T
    w2kvT[D:, :] = proj_ref[2, 2].T
    tailT[0] = outw_ref[1].T
    tailT[1] = ff_ref[1, 0].T
    tailT[2] = ff_ref[1, 1].T
    gains = gain_ref[...].astype(F32)
    for j in range(2):
        column = jnp.broadcast_to(gains[1, j][None, :], (D, D)).T
        gF[j, :, 0:D] = column
        gF[j, :, D:] = column
    q1 = (nn(ind_ref[...], proj_ref[0, 0]) * FACTOR).astype(BF16)
    qBv = jnp.concatenate([q1] * HEADS, axis=0) * bdv
    qB[...] = qBv
    seeds8 = jnp.concatenate([seed_ref[...].astype(F32), jnp.zeros((SP - SEEDS, D), F32)], axis=0)
    seeds16 = jnp.concatenate([seeds8, jnp.zeros((SP, D), F32)], axis=0).astype(BF16)
    q3 = (nn(seeds16, proj_ref[2, 0]) * FACTOR).astype(BF16).astype(F32)[0:SP]
    lane8 = iota((SP, D), 1) // HD
    q3f = jnp.concatenate([jnp.where(lane8 == h, q3, 0.0) for h in range(HEADS)], axis=0)
    q3B[...] = q3f.astype(BF16)
    q3BT[...] = jnp.concatenate([q3f, jnp.zeros((D - HEADS * SP, D), F32)], axis=0).T.astype(BF16)
    gW[0:D, :] = nt(qBv, proj_ref[0, 1]).astype(BF16)
    gW[D:, :] = proj_ref[0, 2].T

    def table(s, start):
        inside = s < set_count
        length = len_ref[jnp.minimum(s, set_count - 1)]
        count = jnp.where(inside, lax.div(length - me + parts - 1, parts), 0)
        starts[s] = start
        counts[s] = count
        return start + count

    lax.fori_loop(0, SLOTS, table, jnp.int32(0))
    pf32[...] = pts_ref[...].astype(F32)
    accg[...] = jnp.zeros_like(accg)
    s1[...] = jnp.zeros_like(s1)
    s3[...] = jnp.zeros_like(s3)

    pl.semaphore_wait(barrier, parts + groups - 2)

    lane256 = iota((1, CR), 1)
    win_row = iota((WIN, D), 0)
    headlane = iota((1, D), 1) // HD

    def phase1(i, carry):
        c = lax.rem(mychunk + 1 + i, NCH)
        pieces = []
        for j in range(CS):
            start = starts[c * CS + j]
            pieces.append(pf32[pl.ds(start, WIN), :])
        x32 = jnp.concatenate(pieces, axis=0)
        x = x32.astype(BF16)
        xt = x32.T.astype(BF16)
        xT[c] = xt
        q2T[c] = (nn(w10T[...], xt) * FACTOR).astype(BF16)
        kv = nn(x, w01kv[...]).astype(BF16)
        v1 = kv[:, D:]
        v1s[c] = v1
        scores = nt(kv[:, 0:D], qB[...])
        numers, ms, dens = [], [], []
        for j in range(CS):
            inside = win_row < counts[c * CS + j]
            sj = jnp.where(inside, scores[j * WIN : (j + 1) * WIN], NEG)
            mj = jnp.max(sj, axis=0, keepdims=True)
            tj = jnp.where(inside, sj - mj, NEG)
            t1s[c, j * WIN : (j + 1) * WIN, :] = tj
            p = jnp.exp(tj)
            ms.append(mj)
            dens.append(jnp.sum(p, axis=0, keepdims=True))
            full = tn(p.astype(BF16), v1[j * WIN : (j + 1) * WIN]).reshape(HEADS, IND, D)
            num = jnp.zeros((IND, D), F32)
            for h in range(HEADS):
                num = num + jnp.where(headlane == h, full[h], 0.0)
            numers.append(num)
        send1[pl.ds(pl.multiple_of(c * (CS * IND), CS * IND), CS * IND), :] = jnp.concatenate(numers, axis=0).astype(BF16)
        for o in range(opc):
            owner = c * opc + o
            blank = [jnp.zeros((4 - spo, D), F32)] if spo < 4 else []
            block = jnp.concatenate(ms[o * spo : (o + 1) * spo] + blank + dens[o * spo : (o + 1) * spo] + blank, axis=0)
            send1m[owner] = block
            rows = pl.ds(pl.multiple_of(owner * ro, ro), ro)

            @pl.when(owner != me)
            def _():
                copy(RS1N, send1.at[rows], recv1.at[me], owner, me).start()
                copy(RS1M, send1m.at[owner], recv1m.at[me], owner, me).start()

            @pl.when(owner == me)
            def _():
                recv1[me] = send1[rows, :]
                recv1m[me] = block

        return carry

    lax.fori_loop(0, NCH, phase1, 0)

    for k in range(1, parts):
        src = lax.rem(me + k, parts)
        copy(RS1N, recv1.at[src], recv1.at[src], src, src).wait_recv()
        copy(RS1M, recv1m.at[src], recv1m.at[src], src, src).wait_recv()

    def expand(rows):
        rep = jnp.concatenate([diag[...] * rows[s : s + 1] for s in range(spo)], axis=0)
        high, low = split(rep)
        return nn(jnp.concatenate([high, low], axis=1), ones2[...])

    def segsum(values):
        high, low = split(values)
        return nn(jnp.concatenate([high, low], axis=1), ones2[...])

    def compress(values):
        wide = segsum(values).reshape(spo, IND, D) * diag[...][None]
        return jnp.sum(wide, axis=1)

    top = recv1m[0, 0:spo]
    for j in range(1, parts):
        top = jnp.maximum(top, recv1m[j, 0:spo])
    den = jnp.zeros((spo, D), F32)
    num = jnp.zeros((ro, D), F32)
    for j in range(parts):
        w = jnp.exp(recv1m[j, 0:spo] - top)
        den = den + w * recv1m[j, 4 : 4 + spo]
        wx = expand(w)
        wexp[j] = wx
        num = num + wx * recv1[j].astype(F32)
    rden = 1.0 / jnp.maximum(den, 0.5)
    rdx = expand(rden)
    rdenx[...] = rdx
    att1 = num * rdx
    numtot[...] = att1
    ind32 = ind_ref[...].astype(F32)
    query = jnp.concatenate([ind32] * spo, axis=0)
    xh, r = norm(query + nn(att1.astype(BF16), outw_ref[0]), 1)
    own0[0] = xh
    own0r[0] = r
    h1 = xh * gains[0, 0][None, :]
    pre = nn(h1.astype(BF16), ff_ref[0, 0])
    own0[1] = pre
    xh, r = norm(h1 + nn(gelu(pre).astype(BF16), ff_ref[0, 1]), 1)
    own0[2] = xh
    own0r[1] = r
    k2rows = pl.ds(pl.multiple_of(me * ro, ro), ro)
    k2all[k2rows, :] = (xh * gains[0, 1][None, :]).astype(BF16)
    for k in range(1, parts):
        dst = lax.rem(me + k, parts)
        copy(AG1, k2all.at[k2rows], k2all.at[k2rows], dst, me).start()

    def pair_rhs(values, t):
        v = values[:, t * 2 * WIN : (t + 1) * 2 * WIN]
        left = v * half0[...]
        return jnp.concatenate([left, v - left], axis=0)

    def blocks(rows):
        return [
            jnp.concatenate([rows[j * IND : (j + 1) * IND]] * HEADS, axis=0) * bd[...] for j in range(CS)
        ]

    def lane_sets():
        return [(lane256 >= j * WIN) & (lane256 < (j + 1) * WIN) for j in range(CS)]

    def phase3(i, carry):
        c = lax.rem(mychunk + i, NCH)
        for o in range(opc):
            owner = c * opc + o

            @pl.when(owner != me)
            def _():
                rows = pl.ds(pl.multiple_of(owner * ro, ro), ro)
                copy(AG1, k2all.at[rows], k2all.at[rows], owner, owner).wait_recv()

        k2c = k2all[pl.ds(pl.multiple_of(c * (CS * IND), CS * IND), CS * IND), :]
        kv2 = nn(k2c, w1kv[...]).astype(BF16)
        kv2s[c] = kv2
        kb = blocks(kv2[:, 0:D])
        vb = blocks(kv2[:, D:])
        q2 = q2T[c]
        sc = [
            nn(jnp.concatenate([kb[2 * t], kb[2 * t + 1]], axis=1), pair_rhs(q2, t)) for t in range(CS // 2)
        ]
        s = jnp.concatenate(sc, axis=1).reshape(HEADS, IND, CR)
        t2 = s - jnp.max(s, axis=1, keepdims=True)
        t2s[c] = t2.reshape(D, CR)
        p = jnp.exp(t2)
        den2 = jnp.sum(p, axis=1, keepdims=True)
        rden2 = 1.0 / den2
        den2s[c] = rden2
        pb = p.reshape(D, CR).astype(BF16)
        nm = [
            tn(jnp.concatenate([vb[2 * t], vb[2 * t + 1]], axis=0), pair_rhs(pb, t)) for t in range(CS // 2)
        ]
        att = (jnp.concatenate(nm, axis=1).reshape(HEADS, HD, CR) * rden2).reshape(D, CR)
        attT[c] = att
        xh, r = norm(xT[c].astype(F32) + nn(tailT[0], att.astype(BF16)), 0)
        xh1s[c] = xh
        r1s[c] = r
        h1 = xh * gF[0]
        pre = nn(tailT[1], h1.astype(BF16))
        ps[c] = pre
        xh, r = norm(h1 + nn(tailT[2], gelu(pre).astype(BF16)), 0)
        xh2s[c] = xh
        r2s[c] = r
        m2 = (xh * gF[1]).astype(BF16)
        m2b[c] = m2
        kv3 = nn(w2kvT[...], m2).astype(BF16)
        kv3T[c] = kv3
        s3 = nn(q3B[...], kv3[0:D])
        sets = lane_sets()
        tops, mrep = [], jnp.zeros((HEADS * SP, CR), F32)
        valid = None
        for j in range(CS):
            live = (lane256 >= j * WIN) & (lane256 < j * WIN + counts[c * CS + j])
            valid = live if valid is None else (valid | live)
            pair = slice((j // 2) * 2 * WIN, (j // 2 + 1) * 2 * WIN)
            mj = jnp.max(jnp.where(live[:, pair], s3[:, pair], NEG), axis=1, keepdims=True)
            tops.append(mj)
            mrep = jnp.where(sets[j], mj, mrep)
        t3 = jnp.where(valid, s3 - mrep, NEG)
        t3s[c] = t3
        p3 = jnp.exp(t3)
        p3blk = jnp.concatenate([jnp.where(sets[j], p3, 0.0) for j in range(CS)], axis=0)
        full = nt(p3blk.astype(BF16), kv3[D:])
        outs = []
        for j in range(CS):
            pair = slice((j // 2) * 2 * WIN, (j // 2 + 1) * 2 * WIN)
            dj = jnp.sum(p3blk[j * HEADS * SP : (j + 1) * HEADS * SP, pair], axis=1, keepdims=True)
            num8 = jnp.zeros((SP, D), F32)
            m8 = jnp.zeros((SP, D), F32)
            d8 = jnp.zeros((SP, D), F32)
            for h in range(HEADS):
                at = headlane == h
                rows = slice(h * SP, (h + 1) * SP)
                num8 = num8 + jnp.where(at, full[j * HEADS * SP + h * SP : j * HEADS * SP + (h + 1) * SP], 0.0)
                m8 = jnp.where(at, tops[j][rows], m8)
                d8 = jnp.where(at, dj[rows], d8)
            outs.append(num8)
            outs.append(jnp.where(iota((SP, D), 1) % HD < HD // 2, m8, d8))
        send2[pl.ds(pl.multiple_of(c * (CS * 16), CS * 16), CS * 16), :] = jnp.concatenate(outs, axis=0)
        for o in range(opc):
            owner = c * opc + o
            rows = pl.ds(pl.multiple_of(owner * (spo * 16), spo * 16), spo * 16)

            @pl.when(owner != me)
            def _():
                copy(RS2, send2.at[rows], recv2.at[me], owner, me).start()

            @pl.when(owner == me)
            def _():
                recv2[me] = send2[rows, :]

        return carry

    lax.fori_loop(0, NCH, phase3, 0)

    for k in range(1, parts):
        src = lax.rem(me + k, parts)
        copy(RS2, recv2.at[src], recv2.at[src], src, src).wait_recv()

    lane_lo = iota((po, D), 1) % HD < HD // 2

    def unpack2(j):
        got = recv2[j].reshape(spo, 2, SP, D)
        num = got[:, 0].reshape(po, D)
        md = got[:, 1].reshape(po, D)
        m = jnp.where(lane_lo, md, pltpu.roll(md, HD // 2, 1))
        d = jnp.where(lane_lo, pltpu.roll(md, D - HD // 2, 1), md)
        return num, m, d

    got2 = [unpack2(j) for j in range(parts)]
    top3 = got2[0][1]
    for j in range(1, parts):
        top3 = jnp.maximum(top3, got2[j][1])
    w3 = [jnp.exp(got2[j][1] - top3) for j in range(parts)]
    den3 = jnp.zeros((po, D), F32)
    num3 = jnp.zeros((po, D), F32)
    for j in range(parts):
        den3 = den3 + w3[j] * got2[j][2]
        num3 = num3 + w3[j] * got2[j][0]
    rden3 = 1.0 / jnp.maximum(den3, 0.5)
    att3 = num3 * rden3
    att3b = att3.astype(BF16)
    query = jnp.concatenate([seeds8] * spo, axis=0)
    g20, g21 = gains[2, 0][None, :], gains[2, 1][None, :]
    xha, ra = norm(query + nn(att3b, outw_ref[2]), 1)
    h1 = xha * g20
    h1b = h1.astype(BF16)
    pre = nn(h1b, ff_ref[2, 0])
    act, dact = gelu_both(pre)
    actb = act.astype(BF16)
    xhb, rb = norm(h1 + nn(actb, ff_ref[2, 1]), 1)
    poolrow[...] = xhb * g21
    cots = []
    for j in range(spo):
        place = me * spo + j
        cj = cot_ref[jnp.minimum(place, set_count - 1)].astype(F32)
        cj = jnp.where(place < set_count, cj, 0.0)
        cots += [cj, jnp.zeros((SP - SEEDS, D), F32)]
    d_out = jnp.concatenate(cots, axis=0)
    d_b = norm_back(d_out, g21, xhb, rb, 1)
    d_bb = d_b.astype(BF16)
    d_pre = (dact * nt(d_bb, ff_ref[2, 1])).astype(BF16)
    d_h1 = d_b + nt(d_pre, ff_ref[2, 0])
    d_c = norm_back(d_h1, g20, xha, ra, 1)
    d_cb = d_c.astype(BF16)
    d_att = nt(d_cb, outw_ref[2])
    dden = -segsum(d_att * att3) * rden3
    total_e = jnp.zeros((po, D), F32)
    eprod = jnp.zeros((po, D), F32)
    dnums = []
    for j in range(parts):
        dn = (w3[j] * (d_att * rden3)).astype(BF16)
        dnums.append(dn)
        eprod = eprod + dn.astype(F32) * got2[j][0]
        total_e = total_e + w3[j] * dden * got2[j][2]
    total_e = total_e + segsum(eprod)
    within = iota((po, D), 1) % HD
    for j in range(parts):
        dd = w3[j] * dden
        high = dd.astype(BF16).astype(F32)
        aux = jnp.where(within == 0, high, jnp.where(within == 1, dd - high, 0.0))
        aux = aux + jnp.where((within == 2) & (got2[j][1] == top3), total_e, 0.0)
        both = jnp.concatenate(
            [dnums[j].astype(F32).reshape(spo, 1, SP, D), aux.reshape(spo, 1, SP, D)], axis=1
        ).reshape(spo * 16, D)
        send2b[j] = both.astype(BF16)
    for k in range(1, parts):
        dst = lax.rem(me + k, parts)
        copy(AG2, send2b.at[dst], recv2b.at[me], dst, me).start()
    recv2b[me] = send2b[me]
    poolall[me] = poolrow[...]
    for k in range(1, parts):
        dst = lax.rem(me + k, parts)
        copy(AGP, poolrow, poolall.at[me], dst, me).start()
    s1[8 * D : 9 * D] = tn(att3b, d_cb)
    s1[9 * D : 10 * D] = tn(h1b, d_pre)
    s1[10 * D : 11 * D] = tn(actb, d_bb)
    s1[11 * D + 8 : 11 * D + 16] = jnp.sum(d_c.reshape(spo, SP, D), axis=0)
    s1[11 * D + 24 : 11 * D + 25] = jnp.sum(d_h1 * xha, axis=0, keepdims=True)
    s1[11 * D + 25 : 11 * D + 26] = jnp.sum(d_out * xhb, axis=0, keepdims=True)

    auxlane = iota((D, D), 0) % HD
    pick_d = jnp.where(auxlane < 2, 1.0, 0.0).astype(BF16)
    pick_e = jnp.where(auxlane == 2, 1.0, 0.0).astype(BF16)

    def phase5(i, carry):
        c = lax.rem(mychunk + i, NCH)
        for o in range(opc):
            owner = c * opc + o

            @pl.when(owner != me)
            def _():
                copy(AG2, recv2b.at[owner], recv2b.at[owner], owner, owner).wait_recv()

        got = recv2b[pl.ds(c * opc, opc)].astype(F32).reshape(CS, 2, SP, D)
        sets = lane_sets()

        def heads(values):
            return jnp.concatenate(
                [jnp.where(headlane == h, values[j], 0.0) for j in range(CS) for h in range(HEADS)], axis=0
            ).astype(BF16)

        d3 = heads(got[:, 0])
        aux3 = heads(got[:, 1])
        kv3 = kv3T[c]
        rhs = jnp.concatenate([kv3[D:], jnp.concatenate([pick_d, pick_d], axis=1)], axis=0)
        dp_all = nn(jnp.concatenate([d3, aux3], axis=1), rhs)
        e_all = nn(aux3, pick_e)
        dp = jnp.zeros((HEADS * SP, CR), F32)
        er = jnp.zeros((HEADS * SP, CR), F32)
        for j in range(CS):
            rows = slice(j * HEADS * SP, (j + 1) * HEADS * SP)
            dp = jnp.where(sets[j], dp_all[rows], dp)
            er = jnp.where(sets[j], jnp.concatenate([e_all[rows], e_all[rows]], axis=1), er)
        t3 = t3s[c]
        p3 = jnp.exp(t3)
        ds3 = (p3 * dp - jnp.where(t3 == 0.0, er, 0.0)).astype(BF16)
        dk3 = nn(q3BT[:, 0 : HEADS * SP], ds3)
        p3blk = jnp.concatenate([jnp.where(sets[j], p3, 0.0) for j in range(CS)], axis=0).astype(BF16)
        dv3 = tn(d3, p3blk)
        dkv3 = jnp.concatenate([dk3, dv3], axis=0).astype(BF16)
        accg[2, 0 : HEADS * SP, 0:D] += nt(ds3, kv3[0:D])
        m2 = m2b[c]
        dw = nt(m2, dkv3)
        s1[3 * D : 4 * D] += dw[:, 0:D]
        s1[4 * D : 5 * D] += dw[:, D:]
        d_m = nn(w2kv[...], dkv3)
        xh2 = xh2s[c]
        accg[1] += d_m * xh2
        d_b = norm_back(d_m, gF[1], xh2, r2s[c], 0)
        d_bb = d_b.astype(BF16)
        act, dact = gelu_both(ps[c])
        s1[7 * D : 8 * D] += nt(act.astype(BF16), d_bb)
        d_pre = (dact * nn(ff_ref[1, 1], d_bb)).astype(BF16)
        xh1 = xh1s[c]
        s1[6 * D : 7 * D] += nt((xh1 * gF[0]).astype(BF16), d_pre)
        d_h1 = d_b + nn(ff_ref[1, 0], d_pre)
        accg[0] += d_h1 * xh1
        d_c = norm_back(d_h1, gF[0], xh1, r1s[c], 0)
        d_cb = d_c.astype(BF16)
        att = attT[c]
        s1[5 * D : 6 * D] += nt(att.astype(BF16), d_cb)
        d_att = nn(outw_ref[1], d_cb)
        rden2 = den2s[c]
        d_num = (d_att.reshape(HEADS, HD, CR) * rden2).reshape(D, CR).astype(BF16)
        dden = -jnp.sum((d_att * att).reshape(HEADS, HD, CR), axis=1, keepdims=True) * rden2
        kv2 = kv2s[c]
        kb = blocks(kv2[:, 0:D])
        vb = blocks(kv2[:, D:])
        dnr = [pair_rhs(d_num, t) for t in range(CS // 2)]
        dp = [
            nn(jnp.concatenate([vb[2 * t], vb[2 * t + 1]], axis=1), dnr[t]) for t in range(CS // 2)
        ]
        t2 = t2s[c].reshape(HEADS, IND, CR)
        p = jnp.exp(t2)
        e = p * (jnp.concatenate(dp, axis=1).reshape(HEADS, IND, CR) + dden)
        ds = (e - jnp.where(t2 == 0.0, jnp.sum(e, axis=1, keepdims=True), 0.0)).reshape(D, CR).astype(BF16)
        pb = p.reshape(D, CR).astype(BF16)
        dsr = [pair_rhs(ds, t) for t in range(CS // 2)]
        dq = [
            tn(jnp.concatenate([kb[2 * t], kb[2 * t + 1]], axis=0), dsr[t]) for t in range(CS // 2)
        ]
        dq = (jnp.concatenate(dq, axis=1) * FACTOR).astype(BF16)
        s1[0:D] += nt(xT[c], dq)
        dxT[c] = d_c + nn(proj_ref[1, 0], dq)
        q2 = q2T[c]
        dks, dvs = [], []
        for t in range(CS // 2):
            lanes = slice(t * 2 * WIN, (t + 1) * 2 * WIN)
            kfull = nt(dsr[t], q2[:, lanes]).reshape(2, HEADS, IND, D)
            vfull = nt(pair_rhs(pb, t), d_num[:, lanes]).reshape(2, HEADS, IND, D)
            for j in range(2):
                dk = jnp.zeros((IND, D), F32)
                dv = jnp.zeros((IND, D), F32)
                for h in range(HEADS):
                    dk = dk + jnp.where(headlane == h, kfull[j, h], 0.0)
                    dv = dv + jnp.where(headlane == h, vfull[j, h], 0.0)
                dks.append(dk)
                dvs.append(dv)
        dkv2 = jnp.concatenate([jnp.concatenate(dks, axis=0), jnp.concatenate(dvs, axis=0)], axis=1).astype(BF16)
        crows = pl.ds(pl.multiple_of(c * (CS * IND), CS * IND), CS * IND)
        send3[crows, :] = nt(dkv2, w1kv[...]).astype(BF16)
        for o in range(opc):
            owner = c * opc + o
            rows = pl.ds(pl.multiple_of(owner * ro, ro), ro)

            @pl.when(owner != me)
            def _():
                copy(RS3, send3.at[rows], recv3.at[me], owner, me).start()

            @pl.when(owner == me)
            def _():
                recv3[me] = send3[rows, :]

        dw = tn(k2all[crows, :], dkv2)
        s1[D : 2 * D] += dw[:, 0:D]
        s1[2 * D : 3 * D] += dw[:, D:]
        return carry

    lax.fori_loop(0, NCH, phase5, 0)

    def slab_start(which, f32_ref, b_ref, r_ref):
        rows = b_ref.shape[1]
        b_ref[...] = f32_ref[...].reshape(b_ref.shape).astype(BF16)
        for k in range(1, parts):
            dst = lax.rem(me + k, parts)
            copy(GRS + which, b_ref.at[dst], r_ref.at[me], dst, me).start()
        r_ref[me] = b_ref[me]

    def slab_mid(which, r_ref, m_ref, mr_ref):
        for k in range(1, parts):
            src = lax.rem(me + k, parts)
            copy(GRS + which, r_ref.at[src], r_ref.at[src], src, src).wait_recv()
        total = r_ref[0].astype(F32)
        for j in range(1, parts):
            total = total + r_ref[j].astype(F32)
        m_ref[...] = total.astype(BF16)
        for k in range(1, groups):
            dst = lax.rem(mine + k, groups)
            gcopy(which, m_ref, mr_ref.at[mine], dst, mine).start()
        mr_ref[mine] = m_ref[...]

    def slab_gather(which, mr_ref, g_ref):
        for k in range(1, groups):
            src = lax.rem(mine + k, groups)
            gcopy(which, mr_ref.at[src], mr_ref.at[src], src, src).wait_recv()
        total = mr_ref[0].astype(F32)
        for j in range(1, groups):
            total = total + mr_ref[j].astype(F32)
        g_ref[me] = total.astype(BF16)
        for k in range(1, parts):
            dst = lax.rem(me + k, parts)
            copy(GAG + which, g_ref.at[me], g_ref.at[me], dst, me).start()

    def slab_finish(which, g_ref):
        for k in range(1, parts):
            src = lax.rem(me + k, parts)
            copy(GAG + which, g_ref.at[src], g_ref.at[src], src, src).wait_recv()
        return g_ref[...].reshape(-1, D).astype(F32)

    qsum = accg[2, 0 : HEADS * SP, 0:D]
    dq3 = jnp.zeros((SP, D), F32)
    for h in range(HEADS):
        dq3 = dq3 + jnp.where(headlane == h, qsum[h * SP : (h + 1) * SP], 0.0)
    s1[11 * D : 11 * D + 8] = dq3
    for j in range(2):
        col = accg[j]
        s1[11 * D + 16 + j : 11 * D + 17 + j] = jnp.sum((col[:, 0:D] + col[:, D:]).T, axis=0, keepdims=True)
    slab_start(0, s1, s1b, s1r)

    for k in range(1, parts):
        src = lax.rem(me + k, parts)
        copy(RS3, recv3.at[src], recv3.at[src], src, src).wait_recv()
    d_out = recv3[0].astype(F32)
    for j in range(1, parts):
        d_out = d_out + recv3[j].astype(F32)
    g00, g01 = gains[0, 0][None, :], gains[0, 1][None, :]
    xha, pre, xhb = own0[0], own0[1], own0[2]
    d_b = norm_back(d_out, g01, xhb, own0r[1], 1)
    d_bb = d_b.astype(BF16)
    act, dact = gelu_both(pre)
    d_pre = (dact * nt(d_bb, ff_ref[0, 1])).astype(BF16)
    d_h1 = d_b + nt(d_pre, ff_ref[0, 0])
    d_c = norm_back(d_h1, g00, xha, own0r[0], 1)
    d_cb = d_c.astype(BF16)
    d_att = nt(d_cb, outw_ref[0])
    att1 = numtot[...]
    d_scaled = d_att * rdenx[...]
    top = recv1m[0, 0:spo]
    for j in range(1, parts):
        top = jnp.maximum(top, recv1m[j, 0:spo])
    ws = [jnp.exp(recv1m[j, 0:spo] - top) for j in range(parts)]
    den = jnp.zeros((spo, D), F32)
    for j in range(parts):
        den = den + ws[j] * recv1m[j, 4 : 4 + spo]
    dden = -compress(d_att * att1) / jnp.maximum(den, 0.5)
    eprod = jnp.zeros((ro, D), F32)
    total_e = dden * den
    for j in range(parts):
        dn = (wexp[j] * d_scaled).astype(BF16)
        send3b[j] = dn
        eprod = eprod + dn.astype(F32) * recv1[j].astype(F32)
    total_e = total_e + compress(eprod)
    for j in range(parts):
        mj = recv1m[j, 0:spo]
        blank = [jnp.zeros((4 - spo, D), F32)] if spo < 4 else []
        send3m[j] = jnp.concatenate(
            [ws[j] * dden] + blank + [jnp.where(mj == top, total_e, 0.0)] + blank, axis=0
        )
    for k in range(1, parts):
        dst = lax.rem(me + k, parts)
        copy(AG3N, send3b.at[dst], recv3b.at[pl.ds(pl.multiple_of(me * ro, ro), ro)], dst, me).start()
        copy(AG3M, send3m.at[dst], recv3m.at[me], dst, me).start()
    recv3b[pl.ds(pl.multiple_of(me * ro, ro), ro), :] = send3b[me]
    recv3m[me] = send3m[me]
    s2[0:D] = tn(att1.astype(BF16), d_cb)
    s2[D : 2 * D] = tn((xha * g00).astype(BF16), d_pre)
    s2[2 * D : 3 * D] = tn(act.astype(BF16), d_bb)
    s2[3 * D :] = jnp.zeros((s2.shape[0] - 3 * D, D), F32)
    s2[3 * D : 3 * D + IND] = jnp.sum(d_c.reshape(spo, IND, D), axis=0)
    s2[3 * D + IND : 3 * D + IND + 1] = jnp.sum(d_h1 * xha, axis=0, keepdims=True)
    s2[3 * D + IND + 1 : 3 * D + IND + 2] = jnp.sum(d_out * xhb, axis=0, keepdims=True)
    slab_mid(0, s1r, s1m, s1mr)
    slab_start(1, s2, s2b, s2r)

    def phase7(i, carry):
        c = lax.rem(mychunk + i, NCH)
        for o in range(opc):
            owner = c * opc + o

            @pl.when(owner != me)
            def _():
                rows = pl.ds(pl.multiple_of(owner * ro, ro), ro)
                copy(AG3N, recv3b.at[rows], recv3b.at[rows], owner, owner).wait_recv()
                copy(AG3M, recv3m.at[owner], recv3m.at[owner], owner, owner).wait_recv()

        dn = recv3b[pl.ds(pl.multiple_of(c * (CS * IND), CS * IND), CS * IND), :]
        db = blocks(dn)
        v1 = v1s[c]
        dss, dvs = [], []
        for j in range(CS):
            rows = slice(j * WIN, (j + 1) * WIN)
            dp = nt(v1[rows], db[j])
            t = t1s[c, rows, :]
            aux = recv3m[c * opc + j // spo]
            q = j % spo
            p = jnp.exp(t)
            e = p * (dp + aux[q : q + 1])
            dss.append((e - jnp.where(t == 0.0, aux[4 + q : 5 + q], 0.0)).astype(BF16))
            dvs.append(nn(p.astype(BF16), db[j]).astype(BF16))
        dsdv = jnp.concatenate([jnp.concatenate(dss, axis=0), jnp.concatenate(dvs, axis=0)], axis=1)
        dw = nn(xT[c], dsdv)
        s3[0:D] += dw[:, 0:D]
        s3[D : 2 * D] += dw[:, D:]
        pgpad[pl.ds(pl.multiple_of(c * CR, CR), CR), :] = nn(dsdv, gW[...]) + dxT[c].T
        return carry

    lax.fori_loop(0, NCH, phase7, 0)
    slab_start(2, s3, s3b, s3r)
    slab_gather(0, s1mr, s1g)
    slab_mid(1, s2r, s2m, s2mr)

    sub8 = iota((8, D), 0)

    def unpad(t, a):
        def half(at, a):
            b = jnp.minimum(a + 1, SLOTS - 1)
            end = starts[b]
            first = pgpad[pl.ds(jnp.minimum(a * WIN + at - starts[a], SLOTS * WIN - 8), 8), :]
            second = pgpad[pl.ds(jnp.minimum(b * WIN + at - end, SLOTS * WIN - 8), 8), :]
            return jnp.where(at + sub8 < end, first, second), jnp.where((end <= at + 8) & (a < SLOTS - 1), a + 1, a)

        lo, a = half(t * 16, a)
        hi, a = half(t * 16 + 8, a)
        pg_o[pl.ds(pl.multiple_of(t * 16, 16), 16), :] = jnp.concatenate([lo, hi], axis=0).astype(BF16)
        return a

    lax.fori_loop(0, pg_o.shape[0] // 16, unpad, jnp.int32(0))

    slab_mid(2, s3r, s3m, s3mr)
    slab_gather(1, s2mr, s2g)

    def halves_product(left, right, dims):
        high, low = split(left)
        return (
            lax.dot_general(high, right, dims, preferred_element_type=F32)
            + lax.dot_general(low, right, dims, preferred_element_type=F32)
        )

    NT_DIMS = (((1,), (1,)), ((), ()))
    TN_DIMS = (((0,), (0,)), ((), ()))

    slab = slab_finish(0, s1g)
    projg_o[1, 0] = slab[0:D]
    projg_o[1, 1] = slab[D : 2 * D]
    projg_o[1, 2] = slab[2 * D : 3 * D]
    projg_o[2, 1] = slab[3 * D : 4 * D]
    projg_o[2, 2] = slab[4 * D : 5 * D]
    outg_o[1] = slab[5 * D : 6 * D]
    ffg_o[1, 0] = slab[6 * D : 7 * D]
    ffg_o[1, 1] = slab[7 * D : 8 * D]
    outg_o[2] = slab[8 * D : 9 * D]
    ffg_o[2, 0] = slab[9 * D : 10 * D]
    ffg_o[2, 1] = slab[10 * D : 11 * D]
    misc = slab[11 * D : 12 * D]
    gaing_o[1] = misc[16:18]
    gaing_o[2] = misc[24:26]
    dq3 = jnp.concatenate([misc[0:8] * FACTOR, jnp.zeros((8, D), F32)], axis=0)
    seedg_o[...] = (halves_product(dq3, proj_ref[2, 0], NT_DIMS)[0:SP] + misc[8:16])[0:SEEDS]
    high, low = split(dq3)
    projg_o[2, 0] = tn(seeds16, high) + tn(seeds16, low)

    slab_gather(2, s3mr, s3g)
    for k in range(1, parts):
        src = lax.rem(me + k, parts)
        copy(AGP, poolall.at[src], poolall.at[src], src, src).wait_recv()
    rows = poolall[...].reshape(SLOTS, SP, D)
    pool_o[...] = rows[0:set_count, 0:SEEDS].astype(BF16)

    slab = slab_finish(1, s2g)
    outg_o[0] = slab[0:D]
    ffg_o[0, 0] = slab[D : 2 * D]
    ffg_o[0, 1] = slab[2 * D : 3 * D]
    misc = slab[3 * D : 4 * D]
    gaing_o[0] = misc[IND : IND + 2]

    slab_finish(2, s3g)
    both = s3g[...].reshape(-1, D)
    projg_o[0, 2] = both[D : 2 * D].astype(F32)
    tsum = both[0:D]
    projg_o[0, 1] = nn(tsum, qB[...])
    full = tn(tsum, proj_ref[0, 1]).reshape(HEADS, IND, D)
    dq1 = jnp.zeros((IND, D), F32)
    for h in range(HEADS):
        dq1 = dq1 + jnp.where(headlane == h, full[h], 0.0)
    dq1 = dq1 * FACTOR
    indg_o[...] = misc[0:IND] + halves_product(dq1, proj_ref[0, 0], NT_DIMS)
    high, low = split(dq1)
    projg_o[0, 0] = tn(ind_ref[...], high) + tn(ind_ref[...], low)

    for k in range(1, parts):
        dst = lax.rem(me + k, parts)
        copy(RS1N, recv1.at[me], recv1.at[me], dst, me).wait_send()
        copy(RS1M, recv1m.at[me], recv1m.at[me], dst, me).wait_send()
        copy(AG1, k2all.at[k2rows], k2all.at[k2rows], dst, me).wait_send()
        copy(RS2, recv2.at[me], recv2.at[me], dst, me).wait_send()
        copy(AG2, recv2b.at[me], recv2b.at[me], dst, me).wait_send()
        copy(AGP, poolrow, poolall.at[me], dst, me).wait_send()
        copy(RS3, recv3.at[me], recv3.at[me], dst, me).wait_send()
        copy(AG3N, send3b.at[me], send3b.at[me], dst, me).wait_send()
        copy(AG3M, recv3m.at[me], recv3m.at[me], dst, me).wait_send()
        for which, (b_ref, g_ref) in enumerate(((s1b, s1g), (s2b, s2g), (s3b, s3g))):
            copy(GRS + which, b_ref.at[me], b_ref.at[me], dst, me).wait_send()
            copy(GAG + which, g_ref.at[me], g_ref.at[me], dst, me).wait_send()
    for k in range(1, groups):
        dst = lax.rem(mine + k, groups)
        for which, m_ref in enumerate((s1m, s2m, s3m)):
            gcopy(which, m_ref, m_ref, dst, mine).wait_send()


def local(parts, groups, points, set_lengths, projections, outputs, feedforward, gains, inducing, seeds, cotangent):
    set_count = set_lengths.shape[0]
    rows = points.shape[0]
    spo = SLOTS // parts
    cfg = (parts, groups, set_count, spo)
    ro, po = spo * IND, spo * SP
    slabs = [slab_rows(n * D, parts) for n in (12, 4, 2)]

    def vm(shape, kind=F32):
        return pltpu.VMEM(shape, kind)

    def slab(n):
        part = n // parts
        return [
            vm((n, D)), vm((parts, part, D), BF16), vm((parts, part, D), BF16),
            vm((part, D), BF16), vm((groups, part, D), BF16), vm((parts, part, D), BF16),
        ]

    scratch = [
        pltpu.SMEM((SLOTS,), jnp.int32), pltpu.SMEM((SLOTS,), jnp.int32),
        vm((rows, D)), vm((SLOTS * WIN, D)), vm((NCH, D, CR), BF16), vm((NCH, CR, D), BF16), vm((NCH, D, CR), BF16),
        vm((NCH, CR, D)), vm((8, D)), vm((NCH, D, CR)), vm((NCH, HEADS, 1, CR)), vm((NCH, D, CR)), vm((NCH, D, CR)),
        vm((NCH, 1, CR)), vm((NCH, D, CR)), vm((NCH, D, CR)), vm((NCH, 1, CR)), vm((NCH, D, CR), BF16),
        vm((NCH, 2 * D, CR), BF16), vm((NCH, HEADS * SP, CR)), vm((NCH, D, CR)), vm((NCH, CS * IND, 2 * D), BF16),
        vm((D, D), BF16), vm((2 * D, D), BF16), vm((IND, D)), vm((D, D), BF16), vm((2, D, CR)),
        vm((D, 2 * D), BF16), vm((D, 2 * D), BF16), vm((D, D), BF16), vm((2 * D, D), BF16), vm((D, 2 * D), BF16),
        vm((3, D, D), BF16), vm((D, D), BF16), vm((HEADS * SP, D), BF16), vm((D, D), BF16), vm((2 * D, D), BF16),
        vm((SLOTS * IND, D), BF16), vm((parts, 8, D)), vm((parts, ro, D), BF16), vm((parts, 8, D)), vm((SLOTS * IND, D), BF16),
        vm((SLOTS * 16, D)), vm((parts, spo * 16, D)), vm((parts, spo * 16, D), BF16), vm((parts, spo * 16, D), BF16),
        vm((po, D)), vm((parts, po, D)),
        vm((SLOTS * IND, D), BF16), vm((parts, ro, D), BF16), vm((parts, ro, D), BF16), vm((SLOTS * IND, D), BF16),
        vm((parts, 8, D)), vm((parts, 8, D)),
        vm((parts, ro, D)), vm((ro, D)), vm((ro, D)), vm((3, ro, D)), vm((2, ro, 1)), vm((8, D)),
        *slab(slabs[0]), *slab(slabs[1]), *slab(slabs[2]),
        vm((3, D, CR)),
        pltpu.SemaphoreType.DMA((PHASES, parts)), pltpu.SemaphoreType.DMA((PHASES, parts)),
        pltpu.SemaphoreType.DMA((3, groups)), pltpu.SemaphoreType.DMA((3, groups)),
    ]
    vmem = pl.BlockSpec(memory_space=pltpu.VMEM)
    out_shape = [
        jax.ShapeDtypeStruct((set_count, SEEDS, D), BF16),
        jax.ShapeDtypeStruct((rows, D), BF16),
        jax.ShapeDtypeStruct((3, 3, D, D), F32),
        jax.ShapeDtypeStruct((3, D, D), F32),
        jax.ShapeDtypeStruct((3, 2, D, D), F32),
        jax.ShapeDtypeStruct((3, 2, D), F32),
        jax.ShapeDtypeStruct((IND, D), F32),
        jax.ShapeDtypeStruct((SEEDS, D), F32),
    ]
    return tuple(
        pl.pallas_call(
            functools.partial(kernel, cfg),
            out_shape=out_shape,
            in_specs=[pl.BlockSpec(memory_space=pltpu.SMEM)] + [vmem] * 8,
            out_specs=[vmem] * 8,
            scratch_shapes=scratch,
            compiler_params=pltpu.CompilerParams(
                collective_id=0, has_side_effects=True, vmem_limit_bytes=48 * 1024 * 1024
            ),
        )(set_lengths, points, projections, outputs, feedforward, gains, inducing, seeds, cotangent)
    )


def solution(mesh):
    parts, groups = mesh.shape["pts"], mesh.shape["sets"]
    placed = (P(("sets", "pts"), None), P("sets"), P(), P(), P(), P(), P(), P(), P("sets", None, None))
    return jax.shard_map(
        functools.partial(local, parts, groups),
        mesh=mesh,
        in_specs=placed,
        out_specs=(P("sets", None, None), P(("sets", "pts"), None), P(), P(), P(), P(), P(), P()),
        check_vma=False,
    )
```

```python
import functools
import math
import types

import jax
import jax.numpy as jnp
from jax import lax
from jax.experimental import pallas as pl
from jax.experimental.pallas import tpu as pltpu
from jax.sharding import PartitionSpec as P

MESH = pl.DeviceIdType.MESH
F32 = jnp.float32
BF16 = jnp.bfloat16
D = 128
HEADS = 4
HD = 32
IND = 32
SEEDS = 4
PR = 2 * SEEDS
SLOTS = 32
WIN = 64
ROWS = SLOTS * WIN
NEG = -1e30
FACTOR = HD**-0.5
G0 = math.sqrt(2.0 / math.pi)
G1 = 0.044715
NS = {1: 4, 3: 4, 5: 4, 7: 4}

RS1N, RS1M, AG1, C2N, C2M, RS3, AG3N, AG3M = range(8)
PHASES = 8
SLABS = (12, 4, 2)


def nn(a, b):
    return lax.dot_general(a, b, (((1,), (0,)), ((), ())), preferred_element_type=F32)


def nt(a, b):
    return lax.dot_general(a, b, (((1,), (1,)), ((), ())), preferred_element_type=F32)


def tn(a, b):
    return lax.dot_general(a, b, (((0,), (0,)), ((), ())), preferred_element_type=F32)


def split(x):
    high = x.astype(BF16)
    return high, (x - high.astype(F32)).astype(BF16)


def iota(shape, dim):
    return lax.broadcasted_iota(jnp.int32, shape, dim)


def norm(values, axis):
    center = values - jnp.mean(values, axis=axis, keepdims=True)
    scale = lax.rsqrt(jnp.mean(center * center, axis=axis, keepdims=True) + 1e-05)
    return center * scale, scale


def norm_back(d_out, gain, hat, scale, axis):
    scaled = d_out * gain
    first = jnp.mean(scaled, axis=axis, keepdims=True)
    second = jnp.mean(scaled * hat, axis=axis, keepdims=True)
    return scale * (scaled - first - hat * second)


def gelu(v):
    th = jnp.tanh(G0 * (v + G1 * (v * v * v)))
    return 0.5 * v * (1.0 + th)


def gelu_both(v):
    sq = v * v
    th = jnp.tanh(v * (G0 + (G0 * G1) * sq))
    half = 0.5 + 0.5 * th
    return v * half, half + (0.5 * v) * (1.0 - th * th) * (G0 + (3.0 * G0 * G1) * sq)


def plan(parts, groups):
    nh = 2 if SLOTS // parts >= 2 else 1
    sh = SLOTS // nh
    return types.SimpleNamespace(
        parts=parts, groups=groups, nh=nh, sh=sh, spo=sh // parts, np=sh // 2, ro=sh // parts * IND,
        qn=2 * groups, hn=parts // 2,
    )


def slab_rows(mats, cfg):
    unit = 16 * cfg.qn
    return (mats * D + unit - 1) // unit * unit


def scratch_table(cfg):
    table = {}

    def vm(name, shape, kind=F32):
        table[name] = pltpu.VMEM(shape, kind)

    nh, sh, parts, ro, npair = cfg.nh, cfg.sh, cfg.parts, cfg.ro, cfg.np
    table["starts"] = pltpu.SMEM((SLOTS,), jnp.int32)
    table["counts"] = pltpu.SMEM((SLOTS,), jnp.int32)
    vm("pf32", (ROWS, D))
    vm("xpad", (ROWS, D), BF16)
    vm("pgpad", (ROWS, D))
    vm("v1s", (ROWS, D), BF16)
    vm("t1s", (ROWS, D))
    vm("m1l", (SLOTS, D))
    for name in ("t2s", "attT", "xh1s", "ps", "xh2s", "dxT"):
        vm(name, (D, ROWS))
    for name in ("xT", "q2T", "m2b"):
        vm(name, (D, ROWS), BF16)
    vm("kv3T", (2 * D, ROWS), BF16)
    vm("t3s", (HEADS * PR, ROWS))
    vm("rden2s", (HEADS, 1, ROWS))
    vm("r1s", (1, ROWS))
    vm("r2s", (1, ROWS))
    vm("kv2s", (SLOTS * IND, 2 * D), BF16)
    vm("bd", (D, D), BF16)
    vm("ones2", (2 * D, D), BF16)
    vm("diag", (IND, D))
    vm("half0", (D, D), BF16)
    vm("gF", (2, D, D))
    vm("e8", (D, D), BF16)
    vm("c8", (2 * D, D), BF16)
    for name in ("w01kv", "w1kv", "w2kv"):
        vm(name, (D, 2 * D), BF16)
    vm("w2kvT", (2 * D, D), BF16)
    vm("gW", (2 * D, D), BF16)
    vm("w10T", (D, D), BF16)
    vm("tailT", (3, D, D), BF16)
    vm("qB", (D, D), BF16)
    vm("q3B", (HEADS * PR, D), BF16)
    vm("q3BT", (D, D), BF16)
    vm("send1", (SLOTS * IND, D), BF16)
    vm("send1m", (nh, parts, 8, D))
    vm("recv1", (nh, parts, ro, D), BF16)
    vm("recv1m", (nh, parts, 8, D))
    vm("k2all", (SLOTS * IND, D), BF16)
    vm("num3", (SLOTS * SEEDS, D))
    vm("m3c", (nh, HEADS * PR, D))
    vm("d3c", (nh, HEADS * PR, D))
    vm("recv2", (nh, parts, sh * SEEDS, D), BF16)
    vm("recv2m", (nh, parts, npair, D))
    vm("dn3", (SLOTS * SEEDS, D))
    vm("cols3", (nh, D, D))
    vm("send3", (SLOTS * IND, D), BF16)
    vm("recv3", (nh, parts, ro, D), BF16)
    vm("dn1", (SLOTS * IND, D), BF16)
    vm("aux1", (nh, parts, 8, D))
    vm("att1", (nh, ro, D))
    vm("rdenx", (nh, ro, D))
    vm("den1", (nh, 8, D))
    vm("own0", (nh, 3, ro, D))
    vm("own0r", (nh, 2, ro, 1))
    vm("gacc", (2, D, D))
    vm("dq3", (HEADS * PR, D))
    for k, mats in enumerate(SLABS):
        rows = slab_rows(mats, cfg)
        part = rows // cfg.qn
        vm(f"s{k}", (rows, D))
        vm(f"s{k}b", (cfg.qn, part, D), BF16)
        vm(f"s{k}r", (cfg.qn, part, D), BF16)
        vm(f"s{k}h", (cfg.hn, part, D), BF16)
        vm(f"s{k}g", (cfg.qn, part, D), BF16)
    table["in_sem"] = pltpu.SemaphoreType.DMA((9,))
    for name in ("ssem", "rsem"):
        table[name] = pltpu.SemaphoreType.DMA((PHASES * nh, parts))
    for name in ("qs", "qr", "gs", "gr"):
        table[name] = pltpu.SemaphoreType.DMA((len(SLABS), cfg.qn))
    for name in ("hs", "hr"):
        table[name] = pltpu.SemaphoreType.DMA((len(SLABS), cfg.hn))
    return table


IN_NAMES = ("lens", "pts", "proj", "outw", "ff", "gain", "ind", "seed", "cot")
OUT_NAMES = ("pool_o", "pg_o", "projg_o", "outg_o", "ffg_o", "gaing_o", "indg_o", "seedg_o")


def kernel(cfg, set_count, names, *refs):
    n_in, n_out = len(IN_NAMES), len(OUT_NAMES)
    hbm = dict(zip(IN_NAMES, refs[:n_in]))
    r = types.SimpleNamespace(**dict(zip(OUT_NAMES, refs[n_in : n_in + n_out])), **dict(zip(names, refs[n_in + n_out :])))
    parts, groups, nh, sh, spo, npair, ro, qn, hn = (
        cfg.parts, cfg.groups, cfg.nh, cfg.sh, cfg.spo, cfg.np, cfg.ro, cfg.qn, cfg.hn,
    )
    me = lax.axis_index("pts")
    mine = lax.axis_index("sets")
    lo, hi = lax.rem(me, 2), lax.div(me, 2)
    q = mine * 2 + lo

    barrier = pltpu.get_barrier_semaphore()
    for k in range(1, parts):
        pl.semaphore_signal(barrier, inc=1, device_id={"pts": lax.rem(me + k, parts)}, device_id_type=MESH)
    for k in range(1, groups):
        for j in range(2):
            at = {"sets": lax.rem(mine + k, groups), "pts": hi * 2 + j}
            pl.semaphore_signal(barrier, inc=1, device_id=at, device_id_type=MESH)
    peers = parts - 1 + 2 * (groups - 1)

    loads = {
        name: pltpu.make_async_copy(hbm[name], getattr(r, name), r.in_sem.at[j]) for j, name in enumerate(IN_NAMES)
    }
    for name in IN_NAMES:
        loads[name].start()

    def copy(ph, hf, src, dst, dev, slot):
        return pltpu.make_async_remote_copy(
            src_ref=src, dst_ref=dst, send_sem=r.ssem.at[ph * nh + hf, dev], recv_sem=r.rsem.at[ph * nh + hf, slot],
            device_id={"pts": dev}, device_id_type=MESH,
        )

    def qcopy(ss, rs, which, src, dst, dev, slot):
        return pltpu.make_async_remote_copy(
            src_ref=src, dst_ref=dst, send_sem=ss.at[which, dev], recv_sem=rs.at[which, slot],
            device_id={"sets": lax.div(dev, 2), "pts": hi * 2 + lax.rem(dev, 2)}, device_id_type=MESH,
        )

    def hcopy(which, src, dst, dev, slot):
        return pltpu.make_async_remote_copy(
            src_ref=src, dst_ref=dst, send_sem=r.hs.at[which, dev], recv_sem=r.hr.at[which, slot],
            device_id={"pts": dev * 2 + lo}, device_id_type=MESH,
        )

    def others(count, own):
        return [lax.rem(own + k, count) for k in range(1, count)]

    def own_rows(hf, dev, rows):
        return pl.ds(pl.multiple_of(hf * sh * (ro // spo) + dev * rows, rows), rows)

    row128 = iota((D, D), 0)
    lane128 = iota((D, D), 1)
    headlane = iota((1, D), 1) // HD
    same_head = (row128 // HD) == (lane128 // HD)
    bdv = jnp.where(same_head, 1.0, 0.0).astype(BF16)
    r.bd[...] = bdv
    r.ones2[0:D, :] = bdv
    r.ones2[D:, :] = bdv
    r.diag[...] = jnp.where((iota((IND, D), 1) % HD) == iota((IND, D), 0), 1.0, 0.0)
    r.half0[...] = jnp.where(lane128 < WIN, 1.0, 0.0).astype(BF16)

    loads["lens"].wait()

    def table(s, start):
        length = r.lens[jnp.minimum(s, set_count - 1)]
        count = jnp.where(s < set_count, lax.div(length - me + parts - 1, parts), 0)
        r.starts[s] = start
        r.counts[s] = count
        return start + count

    lax.fori_loop(0, SLOTS, table, jnp.int32(0))
    loads["ind"].wait()
    loads["proj"].wait()
    r.w01kv[:, 0:D] = r.proj[0, 1]
    r.w01kv[:, D:] = r.proj[0, 2]
    q1 = (nn(r.ind[...], r.proj[0, 0]) * FACTOR).astype(BF16)
    qBv = jnp.concatenate([q1] * HEADS, axis=0) * bdv
    r.qB[...] = qBv
    loads["pts"].wait()
    r.pf32[...] = r.pts[...].astype(F32)

    def by_head(full):
        out = full[HEADS - 1]
        for h in range(HEADS - 2, -1, -1):
            out = jnp.where(headlane == h, full[h], out)
        return out

    win_row = iota((WIN, D), 0)

    def phase1(s0, ns):
        rows = slice(s0 * WIN, (s0 + ns) * WIN)
        x = jnp.concatenate([r.pf32[pl.ds(r.starts[s], WIN), :] for s in range(s0, s0 + ns)], axis=0).astype(BF16)
        r.xpad[rows, :] = x
        kv = nn(x, r.w01kv[...]).astype(BF16)
        v1 = kv[:, D:]
        r.v1s[rows, :] = v1
        scores = nt(kv[:, 0:D], r.qB[...])
        numers = []
        for j in range(ns):
            s = s0 + j
            inside = win_row < r.counts[s]
            sj = scores[j * WIN : (j + 1) * WIN]
            mj = jnp.max(jnp.where(inside, sj, NEG), axis=0, keepdims=True)
            tj = jnp.where(inside, sj - mj, NEG)
            r.t1s[s * WIN : (s + 1) * WIN, :] = tj
            p = jnp.exp(tj)
            r.m1l[s : s + 1, :] = mj
            hf, owner, at = s // sh, s % sh // spo, s % spo
            r.send1m[hf, owner, at : at + 1, :] = mj
            r.send1m[hf, owner, 4 + at : 5 + at, :] = jnp.sum(p, axis=0, keepdims=True)
            numers.append(by_head(tn(p.astype(BF16), v1[j * WIN : (j + 1) * WIN]).reshape(HEADS, IND, D)))
        r.send1[s0 * IND : (s0 + ns) * IND, :] = jnp.concatenate(numers, axis=0).astype(BF16)

    def send1(hf):
        for dst in others(parts, me):
            copy(RS1N, hf, r.send1.at[own_rows(hf, dst, ro)], r.recv1.at[hf, me], dst, me).start()
            copy(RS1M, hf, r.send1m.at[hf, dst], r.recv1m.at[hf, me], dst, me).start()
        r.recv1[hf, me] = r.send1[own_rows(hf, me, ro), :]
        r.recv1m[hf, me] = r.send1m[hf, me]

    def run(phase, n, hf):
        ns = min(NS[n], sh)
        for s0 in range(hf * sh, (hf + 1) * sh, ns):
            phase(s0, ns)

    run(phase1, 1, 0)
    pl.semaphore_wait(barrier, peers)
    send1(0)
    for hf in range(1, nh):
        run(phase1, 1, hf)
        send1(hf)

    loads["gain"].wait()
    loads["outw"].wait()
    loads["ff"].wait()
    r.w1kv[:, 0:D] = r.proj[1, 1]
    r.w1kv[:, D:] = r.proj[1, 2]
    r.w2kv[:, 0:D] = r.proj[2, 1]
    r.w2kv[:, D:] = r.proj[2, 2]
    r.w10T[...] = r.proj[1, 0].T
    for c in range(ROWS // 256):
        at = slice(c * 256, (c + 1) * 256)
        xt = r.xpad[at, :].T
        r.xT[:, at] = xt
        r.q2T[:, at] = (nn(r.w10T[...], xt) * FACTOR).astype(BF16)
    gains = r.gain[...].astype(F32)
    r.w2kvT[0:D, :] = r.proj[2, 1].T
    r.w2kvT[D:, :] = r.proj[2, 2].T
    r.tailT[0] = r.outw[1].T
    r.tailT[1] = r.ff[1, 0].T
    r.tailT[2] = r.ff[1, 1].T
    for j in range(2):
        r.gF[j] = jnp.broadcast_to(gains[1, j][None, :], (D, D)).T
    r.gW[0:D, :] = nt(r.qB[...], r.proj[0, 1]).astype(BF16)
    r.gW[D:, :] = r.proj[0, 2].T
    x8 = row128 % 32 // PR
    r.e8[...] = jnp.where((x8 == lane128 // HD) & (row128 < 64), 1.0, 0.0).astype(BF16)
    c8 = jnp.where((row128 // HD == lane128 // PR) & (lane128 < 32), 1.0, 0.0).astype(BF16)
    r.c8[0:D, :] = c8
    r.c8[D:, :] = c8
    for s in (r.s0, r.s1, r.s2, r.gacc, r.dq3, r.m3c, r.d3c):
        s[...] = jnp.zeros_like(s)
    loads["seed"].wait()
    loads["cot"].wait()
    seed8 = jnp.concatenate([r.seed[...].astype(F32)] * 2, axis=0)
    seed16 = jnp.concatenate([seed8, seed8], axis=0).astype(BF16)
    q3 = (nn(seed16, r.proj[2, 0]) * FACTOR).astype(BF16).astype(F32)[0:PR]
    q3f = jnp.concatenate([jnp.where(headlane == h, q3, 0.0) for h in range(HEADS)], axis=0)
    r.q3B[...] = q3f.astype(BF16)
    r.q3BT[...] = jnp.concatenate([q3f, jnp.zeros((D - HEADS * PR, D), F32)], axis=0).T.astype(BF16)

    def expand(rows):
        rep = jnp.concatenate([r.diag[...] * rows[s : s + 1] for s in range(rows.shape[0])], axis=0)
        high, low = split(rep)
        return nn(jnp.concatenate([high, low], axis=1), r.ones2[...])

    def compress(values):
        high, low = split(values)
        wide = nn(jnp.concatenate([high, low], axis=1), r.ones2[...])
        return jnp.sum(wide.reshape(-1, IND, D) * r.diag[...][None], axis=1)

    ind32 = r.ind[...].astype(F32)

    def phase2(hf):
        for src in others(parts, me):
            copy(RS1N, hf, r.recv1.at[hf, src], r.recv1.at[hf, src], src, src).wait_recv()
            copy(RS1M, hf, r.recv1m.at[hf, src], r.recv1m.at[hf, src], src, src).wait_recv()
        md = [r.recv1m[hf, j] for j in range(parts)]
        top = functools.reduce(jnp.maximum, [v[0:spo] for v in md])
        ws = [jnp.exp(v[0:spo] - top) for v in md]
        den = functools.reduce(jnp.add, [w * v[4 : 4 + spo] for w, v in zip(ws, md)])
        rden = 1.0 / jnp.maximum(den, 0.5)
        wide = expand(jnp.concatenate([w * rden for w in ws] + [rden], axis=0))
        att = jnp.zeros((ro, D), F32)
        for j in range(parts):
            att = att + wide[j * ro : (j + 1) * ro] * r.recv1[hf, j].astype(F32)
        r.rdenx[hf] = wide[parts * ro :]
        r.den1[hf, 0:spo] = den
        r.den1[hf, 4 : 4 + spo] = top
        r.att1[hf] = att
        query = jnp.concatenate([ind32] * spo, axis=0)
        xh, rs = norm(query + nn(att.astype(BF16), r.outw[0]), 1)
        r.own0[hf, 0] = xh
        r.own0r[hf, 0] = rs
        h1 = xh * gains[0, 0][None, :]
        pre = nn(h1.astype(BF16), r.ff[0, 0])
        r.own0[hf, 1] = pre
        xh, rs = norm(h1 + nn(gelu(pre).astype(BF16), r.ff[0, 1]), 1)
        r.own0[hf, 2] = xh
        r.own0r[hf, 1] = rs
        rows = own_rows(hf, me, ro)
        r.k2all[rows, :] = (xh * gains[0, 1][None, :]).astype(BF16)
        for dst in others(parts, me):
            copy(AG1, hf, r.k2all.at[rows], r.k2all.at[rows], dst, me).start()

    for hf in range(nh):
        phase2(hf)

    def pair_rhs(values, t):
        v = values[:, t * 2 * WIN : (t + 1) * 2 * WIN]
        left = v * r.half0[...]
        return jnp.concatenate([left, v - left], axis=0)

    def blocks(rows, ns):
        return [jnp.concatenate([rows[j * IND : (j + 1) * IND]] * HEADS, axis=0) * r.bd[...] for j in range(ns)]

    def wide_gain(j, n):
        return jnp.concatenate([r.gF[j]] * (n // D), axis=1)

    par_row = iota((HEADS * PR, D), 0) % PR // SEEDS
    lane32 = iota((HEADS * PR, D), 1)

    def phase3(s0, ns):
        n = ns * WIN
        at = slice(s0 * WIN, (s0 + ns) * WIN)
        krows = slice(s0 * IND, (s0 + ns) * IND)
        hf = s0 // sh
        kv2 = nn(r.k2all[krows, :], r.w1kv[...]).astype(BF16)
        r.kv2s[krows, :] = kv2
        kb = blocks(kv2[:, 0:D], ns)
        vb = blocks(kv2[:, D:], ns)
        q2 = r.q2T[:, at]
        sc = [nn(jnp.concatenate([kb[2 * t], kb[2 * t + 1]], axis=1), pair_rhs(q2, t)) for t in range(ns // 2)]
        s = jnp.concatenate(sc, axis=1).reshape(HEADS, IND, n)
        t2 = s - jnp.max(s, axis=1, keepdims=True)
        r.t2s[:, at] = t2.reshape(D, n)
        p = jnp.exp(t2)
        rden2 = 1.0 / jnp.sum(p, axis=1, keepdims=True)
        r.rden2s[:, :, at] = rden2
        pb = p.reshape(D, n).astype(BF16)
        nm = [tn(jnp.concatenate([vb[2 * t], vb[2 * t + 1]], axis=0), pair_rhs(pb, t)) for t in range(ns // 2)]
        att = (jnp.concatenate(nm, axis=1).reshape(HEADS, HD, n) * rden2).reshape(D, n)
        r.attT[:, at] = att
        xh, rs = norm(r.xT[:, at].astype(F32) + nn(r.tailT[0], att.astype(BF16)), 0)
        r.xh1s[:, at] = xh
        r.r1s[:, at] = rs
        h1 = xh * wide_gain(0, n)
        pre = nn(r.tailT[1], h1.astype(BF16))
        r.ps[:, at] = pre
        xh, rs = norm(h1 + nn(r.tailT[2], gelu(pre).astype(BF16)), 0)
        r.xh2s[:, at] = xh
        r.r2s[:, at] = rs
        m2 = (xh * wide_gain(1, n)).astype(BF16)
        r.m2b[:, at] = m2
        kv3 = nn(r.w2kvT[...], m2).astype(BF16)
        r.kv3T[:, at] = kv3
        s3 = nn(r.q3B[...], kv3[0:D])
        for t in range(ns // 2):
            sl = slice(t * D, (t + 1) * D)
            sa = s0 + 2 * t
            live = (lane32 >= par_row * WIN) & (
                lane32 < jnp.where(par_row == 0, r.counts[sa], WIN + r.counts[sa + 1])
            )
            mj = jnp.max(jnp.where(live, s3[:, sl], NEG), axis=1, keepdims=True)
            t3 = jnp.where(live, s3[:, sl] - mj, NEG)
            r.t3s[:, (s0 + 2 * t) * WIN : (s0 + 2 * t + 2) * WIN] = t3
            p3 = jnp.exp(t3)
            dj = jnp.sum(p3, axis=1, keepdims=True)
            pair = (sa % sh) // 2
            r.m3c[hf] = jnp.where(lane32 == pair, mj, r.m3c[hf])
            r.d3c[hf] = jnp.where(lane32 == pair, dj, r.d3c[hf])
            full = nt(p3.astype(BF16), kv3[D:, sl]).reshape(HEADS, PR, D)
            r.num3[sa * SEEDS : sa * SEEDS + PR, :] = by_head(full)

    def send2(hf):
        rows = slice(hf * sh * SEEDS, (hf + 1) * sh * SEEDS)
        zero = jnp.zeros((D - 2 * HEADS * PR, D), F32)
        flat = jnp.concatenate([r.m3c[hf], r.d3c[hf], zero], axis=0).T
        r.recv2[hf, me] = r.num3[rows, :].astype(BF16)
        r.recv2m[hf, me] = flat[0:npair]
        for dst in others(parts, me):
            copy(C2N, hf, r.recv2.at[hf, me], r.recv2.at[hf, me], dst, me).start()
            copy(C2M, hf, r.recv2m.at[hf, me], r.recv2m.at[hf, me], dst, me).start()

    for hf in range(nh):
        for src in others(parts, me):
            rows = own_rows(hf, src, ro)
            copy(AG1, hf, r.k2all.at[rows], r.k2all.at[rows], src, src).wait_recv()
        run(phase3, 3, hf)
        send2(hf)

    n3 = sh * SEEDS
    lane_p = iota((npair, D), 1)
    in32 = lane_p < 32
    diag8 = jnp.where((iota((PR, D), 1) % PR == iota((PR, D), 0)) & (iota((PR, D), 1) < 32), 1.0, 0.0)
    row_set = iota((n3, D), 0) // SEEDS
    g20, g21 = gains[2, 0][None, :], gains[2, 1][None, :]

    def expand8(rows):
        rep = jnp.concatenate([diag8 * rows[t : t + 1] for t in range(rows.shape[0])], axis=0)
        high = rep.astype(BF16).astype(F32)
        return nn((high + pltpu.roll(rep - high, 32, 1)).astype(BF16), r.e8[...])

    def compress8(values):
        high, low = split(values)
        wide = nn(jnp.concatenate([high, low], axis=1), r.c8[...])
        return jnp.sum(wide.reshape(npair, PR, D) * diag8[None], axis=1)

    def phase4(hf):
        for src in others(parts, me):
            copy(C2N, hf, r.recv2.at[hf, src], r.recv2.at[hf, src], src, src).wait_recv()
            copy(C2M, hf, r.recv2m.at[hf, src], r.recv2m.at[hf, src], src, src).wait_recv()
        md = [r.recv2m[hf, j] for j in range(parts)]
        top = functools.reduce(jnp.maximum, md)
        ws = [jnp.where(in32, jnp.exp(jnp.minimum(v - top, 0.0)), 0.0) for v in md]
        den = functools.reduce(jnp.add, [w * pltpu.roll(v, D - 32, 1) for w, v in zip(ws, md)])
        rden = 1.0 / jnp.maximum(den, 0.5)
        wide = expand8(jnp.concatenate([w * rden for w in ws] + [jnp.where(in32, rden, 0.0)], axis=0))
        att = jnp.zeros((n3, D), F32)
        for j in range(parts):
            att = att + wide[j * n3 : (j + 1) * n3] * r.recv2[hf, j].astype(F32)
        rdx = wide[parts * n3 :]
        attb = att.astype(BF16)
        query = jnp.concatenate([seed8] * npair, axis=0)
        xha, ra = norm(query + nn(attb, r.outw[2]), 1)
        h1 = xha * g20
        h1b = h1.astype(BF16)
        pre = nn(h1b, r.ff[2, 0])
        act, dact = gelu_both(pre)
        actb = act.astype(BF16)
        xhb, rb = norm(h1 + nn(actb, r.ff[2, 1]), 1)
        pooled = xhb * g21
        cots = []
        for j in range(sh):
            s = hf * sh + j
            cots.append(r.cot[s].astype(F32) if s < set_count else jnp.zeros((SEEDS, D), F32))
            if s < set_count:
                r.pool_o[s] = pooled[j * SEEDS : (j + 1) * SEEDS].astype(BF16)
        d_out = jnp.concatenate(cots, axis=0)
        d_b = norm_back(d_out, g21, xhb, rb, 1)
        d_bb = d_b.astype(BF16)
        d_pre = (dact * nt(d_bb, r.ff[2, 1])).astype(BF16)
        d_h1 = d_b + nt(d_pre, r.ff[2, 0])
        d_c = norm_back(d_h1, g20, xha, ra, 1)
        d_cb = d_c.astype(BF16)
        d_att = nt(d_cb, r.outw[2])
        dn = (d_att * rdx).astype(BF16).astype(F32)
        r.dn3[hf * n3 : (hf + 1) * n3, :] = dn
        dden = -compress8(d_att * att) * rden
        total_e = den * (compress8(dn * att) + dden)
        cols = jnp.where(
            in32, top, jnp.where(lane_p < 64, pltpu.roll(dden, 32, 1), pltpu.roll(total_e, 64, 1))
        )
        r.cols3[hf] = jnp.concatenate([cols, jnp.zeros((D - npair, D), F32)], axis=0).T
        ownrow = row_set // spo == me
        own = jnp.where(ownrow, 1.0, 0.0)
        ownb = own.astype(BF16)
        r.s0[8 * D : 9 * D] += tn(attb, d_cb * ownb)
        r.s0[9 * D : 10 * D] += tn(h1b, d_pre * ownb)
        r.s0[10 * D : 11 * D] += tn(actb, d_bb * ownb)
        r.s0[11 * D + 8 : 11 * D + 16] += jnp.sum((d_c * own).reshape(npair, PR, D), axis=0)
        r.s0[11 * D + 24 : 11 * D + 25] += jnp.sum(d_h1 * xha * own, axis=0, keepdims=True)
        r.s0[11 * D + 25 : 11 * D + 26] += jnp.sum(d_out * xhb * own, axis=0, keepdims=True)

    def fold(values):
        return functools.reduce(jnp.add, [values[:, k * D : (k + 1) * D] for k in range(values.shape[1] // D)])

    def phase5(s0, ns):
        n = ns * WIN
        at = slice(s0 * WIN, (s0 + ns) * WIN)
        krows = slice(s0 * IND, (s0 + ns) * IND)
        hf = s0 // sh
        kv3 = r.kv3T[:, at]
        ds3s, dv3s = [], []
        for t in range(ns // 2):
            sl = slice(t * D, (t + 1) * D)
            sa = s0 + 2 * t
            pair = (sa % sh) // 2
            dn = r.dn3[sa * SEEDS : sa * SEEDS + PR, :]
            d3 = jnp.concatenate([jnp.where(headlane == h, dn, 0.0) for h in range(HEADS)], axis=0).astype(BF16)
            c3 = r.cols3[hf, 0 : 3 * HEADS * PR, pair : pair + 1]
            delta = r.m3c[hf, :, pair : pair + 1] - c3[0 : HEADS * PR]
            t3 = r.t3s[:, (s0 + 2 * t) * WIN : (s0 + 2 * t + 2) * WIN] + delta
            p3 = jnp.exp(t3)
            e = p3 * (nn(d3, kv3[D:, sl]) + c3[HEADS * PR : 2 * HEADS * PR])
            ds3s.append((e - jnp.where(t3 == 0.0, c3[2 * HEADS * PR :], 0.0)).astype(BF16))
            dv3s.append(tn(d3, p3.astype(BF16)))
        ds3 = jnp.concatenate(ds3s, axis=1)
        dk3 = nn(r.q3BT[:, 0 : HEADS * PR], ds3)
        dkv3 = jnp.concatenate([dk3, jnp.concatenate(dv3s, axis=1)], axis=0).astype(BF16)
        r.dq3[...] += nt(ds3, kv3[0:D])
        m2 = r.m2b[:, at]
        dw = nt(m2, dkv3)
        r.s0[3 * D : 4 * D] += dw[:, 0:D]
        r.s0[4 * D : 5 * D] += dw[:, D:]
        d_m = nn(r.w2kv[...], dkv3)
        xh2 = r.xh2s[:, at]
        r.gacc[1] += fold(d_m * xh2)
        d_b = norm_back(d_m, wide_gain(1, n), xh2, r.r2s[:, at], 0)
        d_bb = d_b.astype(BF16)
        act, dact = gelu_both(r.ps[:, at])
        r.s0[7 * D : 8 * D] += nt(act.astype(BF16), d_bb)
        d_pre = (dact * nn(r.ff[1, 1], d_bb)).astype(BF16)
        xh1 = r.xh1s[:, at]
        g0 = wide_gain(0, n)
        r.s0[6 * D : 7 * D] += nt((xh1 * g0).astype(BF16), d_pre)
        d_h1 = d_b + nn(r.ff[1, 0], d_pre)
        r.gacc[0] += fold(d_h1 * xh1)
        d_c = norm_back(d_h1, g0, xh1, r.r1s[:, at], 0)
        d_cb = d_c.astype(BF16)
        att = r.attT[:, at]
        r.s0[5 * D : 6 * D] += nt(att.astype(BF16), d_cb)
        d_att = nn(r.outw[1], d_cb)
        rden2 = r.rden2s[:, :, at]
        d_num = (d_att.reshape(HEADS, HD, n) * rden2).reshape(D, n).astype(BF16)
        dden = -jnp.sum((d_att * att).reshape(HEADS, HD, n), axis=1, keepdims=True) * rden2
        kv2 = r.kv2s[krows, :]
        kb = blocks(kv2[:, 0:D], ns)
        vb = blocks(kv2[:, D:], ns)
        dp = [nn(jnp.concatenate([vb[2 * t], vb[2 * t + 1]], axis=1), pair_rhs(d_num, t)) for t in range(ns // 2)]
        t2 = r.t2s[:, at].reshape(HEADS, IND, n)
        p = jnp.exp(t2)
        e = p * (jnp.concatenate(dp, axis=1).reshape(HEADS, IND, n) + dden)
        ds = (e - jnp.where(t2 == 0.0, jnp.sum(e, axis=1, keepdims=True), 0.0)).reshape(D, n).astype(BF16)
        pb = p.reshape(D, n).astype(BF16)
        dsr = [pair_rhs(ds, t) for t in range(ns // 2)]
        dq = [tn(jnp.concatenate([kb[2 * t], kb[2 * t + 1]], axis=0), dsr[t]) for t in range(ns // 2)]
        dq = (jnp.concatenate(dq, axis=1) * FACTOR).astype(BF16)
        r.s0[0:D] += nt(r.xT[:, at], dq)
        r.dxT[:, at] = d_c + nn(r.proj[1, 0], dq)
        q2 = r.q2T[:, at]
        dks, dvs = [], []
        for t in range(ns // 2):
            sl = slice(t * D, (t + 1) * D)
            kfull = nt(dsr[t], q2[:, sl]).reshape(2, HEADS, IND, D)
            vfull = nt(pair_rhs(pb, t), d_num[:, sl]).reshape(2, HEADS, IND, D)
            for j in range(2):
                dks.append(by_head(kfull[j]))
                dvs.append(by_head(vfull[j]))
        dkv2 = jnp.concatenate([jnp.concatenate(dks, axis=0), jnp.concatenate(dvs, axis=0)], axis=1).astype(BF16)
        r.send3[krows, :] = nt(dkv2, r.w1kv[...]).astype(BF16)
        dw = tn(r.k2all[krows, :], dkv2)
        r.s0[D : 2 * D] += dw[:, 0:D]
        r.s0[2 * D : 3 * D] += dw[:, D:]

    def send3(hf):
        for dst in others(parts, me):
            copy(RS3, hf, r.send3.at[own_rows(hf, dst, ro)], r.recv3.at[hf, me], dst, me).start()
        r.recv3[hf, me] = r.send3[own_rows(hf, me, ro), :]

    slabs = [tuple(getattr(r, f"s{k}{x}") for x in ("", "b", "r", "h", "g")) for k in range(len(SLABS))]

    def slab_start(which):
        f_ref, b_ref, r_ref, _, _ = slabs[which]
        b_ref[...] = f_ref[...].reshape(b_ref.shape).astype(BF16)
        for dst in others(qn, q):
            qcopy(r.qs, r.qr, which, b_ref.at[dst], r_ref.at[q], dst, q).start()
        r_ref[q] = b_ref[q]

    def slab_mid(which):
        _, _, r_ref, h_ref, _ = slabs[which]
        for src in others(qn, q):
            qcopy(r.qs, r.qr, which, r_ref.at[src], r_ref.at[src], src, src).wait_recv()
        h_ref[hi] = functools.reduce(jnp.add, [r_ref[j].astype(F32) for j in range(qn)]).astype(BF16)
        for dst in others(hn, hi):
            hcopy(which, h_ref.at[hi], h_ref.at[hi], dst, hi).start()

    def slab_gather(which):
        _, _, _, h_ref, g_ref = slabs[which]
        for src in others(hn, hi):
            hcopy(which, h_ref.at[src], h_ref.at[src], src, src).wait_recv()
        g_ref[q] = functools.reduce(jnp.add, [h_ref[j].astype(F32) for j in range(hn)]).astype(BF16)
        for dst in others(qn, q):
            qcopy(r.gs, r.gr, which, g_ref.at[q], g_ref.at[q], dst, q).start()

    def slab_finish(which):
        g_ref = slabs[which][4]
        for src in others(qn, q):
            qcopy(r.gs, r.gr, which, g_ref.at[src], g_ref.at[src], src, src).wait_recv()
        return g_ref[...].reshape(-1, D)

    for hf in range(nh):
        phase4(hf)
        run(phase5, 5, hf)
        send3(hf)

    r.s0[11 * D : 11 * D + 8] = by_head(r.dq3[...].reshape(HEADS, PR, D))
    for j in range(2):
        r.s0[11 * D + 16 + j : 11 * D + 17 + j] = jnp.sum(r.gacc[j].T, axis=0, keepdims=True)
    slab_start(0)

    g00, g01 = gains[0, 0][None, :], gains[0, 1][None, :]

    def phase6(hf):
        for src in others(parts, me):
            copy(RS3, hf, r.recv3.at[hf, src], r.recv3.at[hf, src], src, src).wait_recv()
        d_out = functools.reduce(jnp.add, [r.recv3[hf, j].astype(F32) for j in range(parts)])
        xha, pre, xhb = r.own0[hf, 0], r.own0[hf, 1], r.own0[hf, 2]
        d_b = norm_back(d_out, g01, xhb, r.own0r[hf, 1], 1)
        d_bb = d_b.astype(BF16)
        act, dact = gelu_both(pre)
        d_pre = (dact * nt(d_bb, r.ff[0, 1])).astype(BF16)
        d_h1 = d_b + nt(d_pre, r.ff[0, 0])
        d_c = norm_back(d_h1, g00, xha, r.own0r[hf, 0], 1)
        d_cb = d_c.astype(BF16)
        d_att = nt(d_cb, r.outw[0])
        att = r.att1[hf]
        dn = (d_att * r.rdenx[hf]).astype(BF16)
        rows = own_rows(hf, me, ro)
        r.dn1[rows, :] = dn
        den = r.den1[hf, 0:spo]
        sums = compress(jnp.concatenate([d_att * att, dn.astype(F32) * att], axis=0))
        dden = -sums[0:spo] / jnp.maximum(den, 0.5)
        r.aux1[hf, me, 0:spo] = dden
        r.aux1[hf, me, spo : 2 * spo] = den * (sums[spo:] + dden)
        r.aux1[hf, me, 2 * spo : 3 * spo] = r.den1[hf, 4 : 4 + spo]
        for dst in others(parts, me):
            copy(AG3N, hf, r.dn1.at[rows], r.dn1.at[rows], dst, me).start()
            copy(AG3M, hf, r.aux1.at[hf, me], r.aux1.at[hf, me], dst, me).start()
        r.s1[0:D] += tn(att.astype(BF16), d_cb)
        r.s1[D : 2 * D] += tn((xha * g00).astype(BF16), d_pre)
        r.s1[2 * D : 3 * D] += tn(act.astype(BF16), d_bb)
        r.s1[3 * D : 3 * D + IND] += jnp.sum(d_c.reshape(spo, IND, D), axis=0)
        r.s1[3 * D + IND : 3 * D + IND + 1] += jnp.sum(d_h1 * xha, axis=0, keepdims=True)
        r.s1[3 * D + IND + 1 : 3 * D + IND + 2] += jnp.sum(d_out * xhb, axis=0, keepdims=True)

    for hf in range(nh):
        phase6(hf)
    slab_start(1)
    slab_mid(0)

    def phase7(s0, ns):
        at = slice(s0 * WIN, (s0 + ns) * WIN)
        hf = s0 // sh
        db = blocks(r.dn1[s0 * IND : (s0 + ns) * IND, :], ns)
        dss, dvs = [], []
        for j in range(ns):
            s = s0 + j
            rows = slice(s * WIN, (s + 1) * WIN)
            dp = nt(r.v1s[rows, :], db[j])
            owner, w = s % sh // spo, s % spo
            aux = r.aux1[hf, owner]
            t = r.t1s[rows, :] + (r.m1l[s : s + 1] - aux[2 * spo + w : 2 * spo + w + 1])
            p = jnp.exp(t)
            e = p * (dp + aux[w : w + 1])
            dss.append((e - jnp.where(t == 0.0, aux[spo + w : spo + w + 1], 0.0)).astype(BF16))
            dvs.append(nn(p.astype(BF16), db[j]).astype(BF16))
        dsdv = jnp.concatenate([jnp.concatenate(dss, axis=0), jnp.concatenate(dvs, axis=0)], axis=1)
        dw = nn(r.xT[:, at], dsdv)
        r.s2[0:D] += dw[:, 0:D]
        r.s2[D : 2 * D] += dw[:, D:]
        r.pgpad[at, :] = nn(dsdv, r.gW[...]) + r.dxT[:, at].T

    for hf in range(nh):
        for src in others(parts, me):
            rows = own_rows(hf, src, ro)
            copy(AG3N, hf, r.dn1.at[rows], r.dn1.at[rows], src, src).wait_recv()
            copy(AG3M, hf, r.aux1.at[hf, src], r.aux1.at[hf, src], src, src).wait_recv()
        run(phase7, 7, hf)
    slab_start(2)
    slab_gather(0)
    slab_mid(1)

    sub8 = iota((8, D), 0)

    def unpad(t, a):
        def half(at, a):
            b = jnp.minimum(a + 1, SLOTS - 1)
            end = r.starts[b]
            first = r.pgpad[pl.ds(jnp.minimum(a * WIN + at - r.starts[a], ROWS - 8), 8), :]
            second = r.pgpad[pl.ds(jnp.minimum(b * WIN + at - end, ROWS - 8), 8), :]
            return jnp.where(at + sub8 < end, first, second), jnp.where((end <= at + 8) & (a < SLOTS - 1), a + 1, a)

        upper, a = half(t * 16, a)
        lower, a = half(t * 16 + 8, a)
        r.pg_o[pl.ds(pl.multiple_of(t * 16, 16), 16), :] = jnp.concatenate([upper, lower], axis=0).astype(BF16)
        return a

    lax.fori_loop(0, ROWS // 16, unpad, jnp.int32(0))

    slab_mid(2)
    slab_gather(1)

    def exact(left, right, product):
        high, low = split(left)
        return product(high, right) + product(low, right)

    slab = slab_finish(0)
    mats = [slab[k * D : (k + 1) * D].astype(F32) for k in range(SLABS[0])]
    for k, place in enumerate(((1, 0), (1, 1), (1, 2), (2, 1), (2, 2))):
        r.projg_o[place] = mats[k]
    r.outg_o[1] = mats[5]
    r.ffg_o[1, 0] = mats[6]
    r.ffg_o[1, 1] = mats[7]
    r.outg_o[2] = mats[8]
    r.ffg_o[2, 0] = mats[9]
    r.ffg_o[2, 1] = mats[10]
    misc = mats[11]
    r.gaing_o[1] = misc[16:18]
    r.gaing_o[2] = misc[24:26]
    dq3 = (misc[0:SEEDS] + misc[SEEDS:PR]) * FACTOR
    dq3 = jnp.concatenate([dq3, jnp.zeros((16 - SEEDS, D), F32)], axis=0)
    high, low = split(dq3)
    r.seedg_o[...] = (nt(high, r.proj[2, 0]) + nt(low, r.proj[2, 0]))[0:SEEDS] + misc[8 : 8 + SEEDS] + misc[12:16]
    r.projg_o[2, 0] = tn(seed16, high) + tn(seed16, low)

    slab_gather(2)
    slab = slab_finish(1)
    r.outg_o[0] = slab[0:D].astype(F32)
    r.ffg_o[0, 0] = slab[D : 2 * D].astype(F32)
    r.ffg_o[0, 1] = slab[2 * D : 3 * D].astype(F32)
    misc = slab[3 * D : 4 * D].astype(F32)
    r.gaing_o[0] = misc[IND : IND + 2]

    slab = slab_finish(2)
    r.projg_o[0, 2] = slab[D : 2 * D].astype(F32)
    tsum = slab[0:D]
    r.projg_o[0, 1] = nn(tsum, r.qB[...])
    dq1 = by_head(tn(tsum, r.proj[0, 1]).reshape(HEADS, IND, D)) * FACTOR
    high, low = split(dq1)
    r.indg_o[...] = misc[0:IND] + nt(high, r.proj[0, 0]) + nt(low, r.proj[0, 0])
    r.projg_o[0, 0] = tn(r.ind[...], high) + tn(r.ind[...], low)

    for hf in range(nh):
        rows = own_rows(hf, me, ro)
        for dst in others(parts, me):
            copy(RS1N, hf, r.recv1.at[hf, me], r.recv1.at[hf, me], dst, me).wait_send()
            copy(RS1M, hf, r.recv1m.at[hf, me], r.recv1m.at[hf, me], dst, me).wait_send()
            copy(AG1, hf, r.k2all.at[rows], r.k2all.at[rows], dst, me).wait_send()
            copy(C2N, hf, r.recv2.at[hf, me], r.recv2.at[hf, me], dst, me).wait_send()
            copy(C2M, hf, r.recv2m.at[hf, me], r.recv2m.at[hf, me], dst, me).wait_send()
            copy(RS3, hf, r.recv3.at[hf, me], r.recv3.at[hf, me], dst, me).wait_send()
            copy(AG3N, hf, r.dn1.at[rows], r.dn1.at[rows], dst, me).wait_send()
            copy(AG3M, hf, r.aux1.at[hf, me], r.aux1.at[hf, me], dst, me).wait_send()
    for which, (_, b_ref, _, h_ref, g_ref) in enumerate(slabs):
        for dst in others(qn, q):
            qcopy(r.qs, r.qr, which, b_ref.at[q], b_ref.at[q], dst, q).wait_send()
            qcopy(r.gs, r.gr, which, g_ref.at[q], g_ref.at[q], dst, q).wait_send()
        for dst in others(hn, hi):
            hcopy(which, h_ref.at[hi], h_ref.at[hi], dst, hi).wait_send()


def write_out(*refs):
    n = len(OUT_NAMES)
    sems = refs[2 * n]
    copies = [pltpu.make_async_copy(refs[j], refs[n + j], sems.at[j]) for j in range(n)]
    for c in copies:
        c.start()
    for c in copies:
        c.wait()


def local(parts, groups, points, set_lengths, projections, outputs, feedforward, gains, inducing, seeds, cotangent):
    set_count = set_lengths.shape[0]
    cfg = plan(parts, groups)
    args = (set_lengths, points, projections, outputs, feedforward, gains, inducing, seeds, cotangent)
    table = {}
    for name, a in zip(IN_NAMES, args):
        table[name] = pltpu.SMEM(a.shape, a.dtype) if name == "lens" else pltpu.VMEM(a.shape, a.dtype)
    table.update(scratch_table(cfg))
    vmem = pl.BlockSpec(memory_space=pltpu.VMEM)
    args = tuple(pltpu.with_memory_space_constraint(a, pltpu.HBM) for a in args)
    hbm = pl.BlockSpec(memory_space=pltpu.HBM)
    out_shape = [
        jax.ShapeDtypeStruct((set_count, SEEDS, D), BF16),
        jax.ShapeDtypeStruct(points.shape, BF16),
        jax.ShapeDtypeStruct((3, 3, D, D), F32),
        jax.ShapeDtypeStruct((3, D, D), F32),
        jax.ShapeDtypeStruct((3, 2, D, D), F32),
        jax.ShapeDtypeStruct((3, 2, D), F32),
        jax.ShapeDtypeStruct((IND, D), F32),
        jax.ShapeDtypeStruct((SEEDS, D), F32),
    ]
    n = len(out_shape)
    results = pl.pallas_call(
        functools.partial(kernel, cfg, set_count, tuple(table)),
        out_shape=[pltpu.VMEM(o.shape, o.dtype) for o in out_shape],
        in_specs=[hbm] * len(args),
        out_specs=[vmem] * n,
        scratch_shapes=list(table.values()),
        compiler_params=pltpu.CompilerParams(
            collective_id=0, has_side_effects=True, vmem_limit_bytes=48 * 1024 * 1024
        ),
    )(*args)
    results = [pltpu.with_memory_space_constraint(a, pltpu.VMEM) for a in results]
    return tuple(
        pl.pallas_call(
            write_out,
            out_shape=out_shape,
            in_specs=[vmem] * n,
            out_specs=[hbm] * n,
            scratch_shapes=[pltpu.SemaphoreType.DMA((n,))],
        )(*results)
    )


def solution(mesh):
    parts, groups = mesh.shape["pts"], mesh.shape["sets"]
    placed = (P(("sets", "pts"), None), P("sets"), P(), P(), P(), P(), P(), P(), P("sets", None, None))
    return jax.shard_map(
        functools.partial(local, parts, groups),
        mesh=mesh,
        in_specs=placed,
        out_specs=(P("sets", None, None), P(("sets", "pts"), None), P(), P(), P(), P(), P(), P()),
        check_vma=False,
    )
```

```python
import functools
import math
import types

import jax
import jax.numpy as jnp
from jax import lax
from jax.experimental import pallas as pl
from jax.experimental.pallas import tpu as pltpu
from jax.sharding import PartitionSpec as P

MESH = pl.DeviceIdType.MESH
F32 = jnp.float32
BF16 = jnp.bfloat16
D = 128
HEADS = 4
HD = 32
IND = 32
SEEDS = 4
SP = 8
HS = HEADS * SP
SLOTS = 32
WIN = 64
ROWS = SLOTS * WIN
NEG = -1e30
FACTOR = HD**-0.5
G0 = math.sqrt(2.0 / math.pi)
G1 = 0.044715
SLABS = (12, 6)


def nn(a, b):
    return lax.dot_general(a, b, (((1,), (0,)), ((), ())), preferred_element_type=F32)


def nt(a, b):
    return lax.dot_general(a, b, (((1,), (1,)), ((), ())), preferred_element_type=F32)


def tn(a, b):
    return lax.dot_general(a, b, (((0,), (0,)), ((), ())), preferred_element_type=F32)


def split(x):
    high = x.astype(BF16)
    return high, (x - high.astype(F32)).astype(BF16)


def iota(shape, dim):
    return lax.broadcasted_iota(jnp.int32, shape, dim)


def total(values):
    return functools.reduce(jnp.add, values)


def norm(values, axis):
    center = values - jnp.mean(values, axis=axis, keepdims=True)
    scale = lax.rsqrt(jnp.mean(center * center, axis=axis, keepdims=True) + 1e-05)
    return center * scale, scale


def norm_back(d_out, gain, hat, scale, axis):
    scaled = d_out * gain
    first = jnp.mean(scaled, axis=axis, keepdims=True)
    second = jnp.mean(scaled * hat, axis=axis, keepdims=True)
    return scale * (scaled - first - hat * second)


def gelu(v):
    th = jnp.tanh(G0 * (v + G1 * (v * v * v)))
    return 0.5 * v * (1.0 + th)


def gelu_both(v):
    sq = v * v
    th = jnp.tanh(v * (G0 + (G0 * G1) * sq))
    half = 0.5 + 0.5 * th
    return v * half, half + (0.5 * v) * (1.0 - th * th) * (G0 + (3.0 * G0 * G1) * sq)


def plan(parts, groups):
    spo = SLOTS // parts
    ng = 2 if spo >= 2 else 1
    return types.SimpleNamespace(
        parts=parts, groups=groups, spo=spo, rs=parts * WIN, ng=ng, gsz=spo // ng, qn=2 * groups, hn=parts // 2,
        pool=max(8, spo * SEEDS),
    )


def slab_rows(mats, cfg):
    unit = 16 * cfg.qn
    return (mats * D + unit - 1) // unit * unit


def scratch_table(cfg):
    table = {}

    def vm(name, shape, kind=F32):
        table[name] = pltpu.VMEM(shape, kind)

    spo, parts = cfg.spo, cfg.parts
    table["starts"] = pltpu.SMEM((SLOTS,), jnp.int32)
    vm("pf32", (ROWS, D))
    vm("xs", (spo, parts, WIN, D), BF16)
    vm("xr", (spo, parts, WIN, D), BF16)
    vm("pgs", (spo, parts, WIN, D), BF16)
    vm("pgr", (spo, parts, WIN, D), BF16)
    vm("pgpad", (ROWS, D))
    vm("v1s", (ROWS, D), BF16)
    vm("t1s", (ROWS, D))
    for name in ("t2s", "attT", "xh1s", "ps", "xh2s", "dxT"):
        vm(name, (D, ROWS))
    for name in ("xT", "q2T", "m2b"):
        vm(name, (D, ROWS), BF16)
    vm("kv3T", (2 * D, ROWS), BF16)
    vm("t3s", (HS, ROWS))
    vm("rden2s", (HEADS, 1, ROWS))
    vm("r1s", (1, ROWS))
    vm("r2s", (1, ROWS))
    vm("k2s", (spo * IND, D), BF16)
    vm("kv2s", (spo * IND, 2 * D), BF16)
    vm("num1", (spo * IND, D))
    vm("den1", (spo, D))
    vm("att1", (spo * IND, D))
    vm("rdenx", (spo * IND, D))
    vm("own0", (3, spo * IND, D))
    vm("own0r", (2, spo * IND, 1))
    vm("dk2s", (spo * IND, D))
    vm("dn1", (spo * IND, D), BF16)
    vm("dden1", (spo, D))
    vm("num3", (spo * SP, D))
    vm("rden3", (spo * HS, 1))
    vm("d3s", (spo * HS, D), BF16)
    vm("dd3", (spo * HS, 1))
    vm("poolrow", (cfg.pool, D))
    vm("poolall", (parts, cfg.pool, D))
    vm("bd", (D, D), BF16)
    vm("ones2", (2 * D, D), BF16)
    vm("diag", (IND, D))
    vm("gF", (2, D, D))
    for name in ("w01kv", "w1kv", "w2kv"):
        vm(name, (D, 2 * D), BF16)
    vm("w2kvT", (2 * D, D), BF16)
    vm("gW", (2 * D, D), BF16)
    vm("w10T", (D, D), BF16)
    vm("tailT", (3, D, D), BF16)
    vm("qB", (D, D), BF16)
    vm("q3B", (HS, D), BF16)
    vm("q3BT", (D, D), BF16)
    vm("gacc", (2, D, D))
    vm("dq3", (HS, D))
    for k, mats in enumerate(SLABS):
        rows = slab_rows(mats, cfg)
        part = rows // cfg.qn
        vm(f"s{k}", (rows, D))
        vm(f"s{k}b", (cfg.qn, part, D), BF16)
        vm(f"s{k}r", (cfg.qn, part, D), BF16)
        vm(f"s{k}h", (cfg.hn, part, D), BF16)
        vm(f"s{k}g", (cfg.qn, part, D), BF16)
    table["in_sem"] = pltpu.SemaphoreType.DMA((9,))
    for name in ("ssem", "rsem"):
        table[name] = pltpu.SemaphoreType.DMA((2 * spo + 1, parts))
    for name in ("qs", "qr"):
        table[name] = pltpu.SemaphoreType.DMA((2 * len(SLABS), cfg.qn))
    for name in ("hs", "hr"):
        table[name] = pltpu.SemaphoreType.DMA((len(SLABS), cfg.hn))
    return table


IN_NAMES = ("lens", "pts", "proj", "outw", "ff", "gain", "ind", "seed", "cot")
OUT_NAMES = ("pool_o", "pg_o", "projg_o", "outg_o", "ffg_o", "gaing_o", "indg_o", "seedg_o")


def kernel(cfg, set_count, names, *refs):
    n_in, n_out = len(IN_NAMES), len(OUT_NAMES)
    hbm = dict(zip(IN_NAMES, refs[:n_in]))
    r = types.SimpleNamespace(**dict(zip(OUT_NAMES, refs[n_in : n_in + n_out])), **dict(zip(names, refs[n_in + n_out :])))
    parts, groups, spo, rs, ng, gsz, qn, hn = (
        cfg.parts, cfg.groups, cfg.spo, cfg.rs, cfg.ng, cfg.gsz, cfg.qn, cfg.hn,
    )
    me = lax.axis_index("pts")
    mine = lax.axis_index("sets")
    lo, hi = lax.rem(me, 2), lax.div(me, 2)
    q = mine * 2 + lo

    barrier = pltpu.get_barrier_semaphore()
    for k in range(1, parts):
        pl.semaphore_signal(barrier, inc=1, device_id={"pts": lax.rem(me + k, parts)}, device_id_type=MESH)
    for k in range(1, groups):
        for j in range(2):
            at = {"sets": lax.rem(mine + k, groups), "pts": hi * 2 + j}
            pl.semaphore_signal(barrier, inc=1, device_id=at, device_id_type=MESH)
    peers = parts - 1 + 2 * (groups - 1)

    loads = {
        name: pltpu.make_async_copy(hbm[name], getattr(r, name), r.in_sem.at[j]) for j, name in enumerate(IN_NAMES)
    }
    for name in IN_NAMES:
        loads[name].start()

    leaving, coming = [], {}
    lines = {
        "pts": (parts, me, r.ssem, r.rsem, lambda dev: {"pts": dev}),
        "layer": (qn, q, r.qs, r.qr, lambda dev: {"sets": lax.div(dev, 2), "pts": hi * 2 + lax.rem(dev, 2)}),
        "column": (hn, hi, r.hs, r.hr, lambda dev: {"pts": dev * 2 + lo}),
    }

    def exchange(key, line, index, source, land):
        count, own, send_sem, recv_sem, where = lines[line]
        waits = coming.setdefault(key, [])
        for k in range(1, count):
            dev = lax.rem(own + k, count)
            sent = pltpu.make_async_remote_copy(
                src_ref=source(dev), dst_ref=land(own), send_sem=send_sem.at[index, dev],
                recv_sem=recv_sem.at[index, own], device_id=where(dev), device_id_type=MESH,
            )
            sent.start()
            leaving.append(sent)
            waits.append(
                pltpu.make_async_remote_copy(
                    src_ref=land(dev), dst_ref=land(dev), send_sem=send_sem.at[index, dev],
                    recv_sem=recv_sem.at[index, dev], device_id=where(dev), device_id_type=MESH,
                )
            )

    def arrive(key):
        for wait in coming.pop(key):
            wait.wait_recv()

    def flush():
        for key in list(coming):
            arrive(key)
        for sent in leaving:
            sent.wait_send()

    loads["lens"].wait()

    def table(s, start):
        length = r.lens[jnp.minimum(s, set_count - 1)]
        r.starts[s] = start
        return start + jnp.where(s < set_count, lax.div(length - me + parts - 1, parts), 0)

    lax.fori_loop(0, SLOTS, table, jnp.int32(0))
    loads["pts"].wait()
    r.pf32[...] = r.pts[...].astype(F32)

    def gather(j):
        for o in range(parts):
            r.xs[j, o] = r.pf32[pl.ds(r.starts[o * spo + j], WIN), :].astype(BF16)
        r.xr[j, me] = r.xs[j, me]

    gather(0)
    pl.semaphore_wait(barrier, peers)
    for j in range(spo):
        if j:
            gather(j)
        exchange(("x", j), "pts", j, lambda dev: r.xs.at[j, dev], lambda dev: r.xr.at[j, dev])

    row128 = iota((D, D), 0)
    lane128 = iota((D, D), 1)
    headlane = iota((1, D), 1) // HD
    bdv = jnp.where((row128 // HD) == (lane128 // HD), 1.0, 0.0).astype(BF16)
    r.bd[...] = bdv
    r.ones2[0:D, :] = bdv
    r.ones2[D:, :] = bdv
    r.diag[...] = jnp.where((iota((IND, D), 1) % HD) == iota((IND, D), 0), 1.0, 0.0)
    for name in IN_NAMES[2:]:
        loads[name].wait()
    for a, name in ((0, "w01kv"), (1, "w1kv"), (2, "w2kv")):
        joined = getattr(r, name)
        joined[:, 0:D] = r.proj[a, 1]
        joined[:, D:] = r.proj[a, 2]
    r.w10T[...] = r.proj[1, 0].T
    r.w2kvT[0:D, :] = r.proj[2, 1].T
    r.w2kvT[D:, :] = r.proj[2, 2].T
    r.tailT[0] = r.outw[1].T
    r.tailT[1] = r.ff[1, 0].T
    r.tailT[2] = r.ff[1, 1].T
    gains = r.gain[...].astype(F32)
    for j in range(2):
        r.gF[j] = jnp.broadcast_to(gains[1, j][None, :], (D, D)).T
    q1 = (nn(r.ind[...], r.proj[0, 0]) * FACTOR).astype(BF16)
    r.qB[...] = jnp.concatenate([q1] * HEADS, axis=0) * bdv
    r.gW[0:D, :] = nt(r.qB[...], r.proj[0, 1]).astype(BF16)
    r.gW[D:, :] = r.proj[0, 2].T
    ind32 = r.ind[...].astype(F32)
    seed8 = jnp.concatenate([r.seed[...].astype(F32), jnp.zeros((SP - SEEDS, D), F32)], axis=0)
    seed16 = jnp.concatenate([seed8, jnp.zeros((SP, D), F32)], axis=0).astype(BF16)
    q3 = (nn(seed16, r.proj[2, 0]) * FACTOR).astype(BF16).astype(F32)[0:SP]
    q3f = jnp.concatenate([jnp.where(headlane == h, q3, 0.0) for h in range(HEADS)], axis=0)
    r.q3B[...] = q3f.astype(BF16)
    r.q3BT[...] = jnp.concatenate([q3f, jnp.zeros((D - HS, D), F32)], axis=0).T.astype(BF16)
    for s in (r.s0, r.s1, r.gacc, r.dq3, r.poolrow):
        s[...] = jnp.zeros_like(s)

    def length_of(j):
        s = me * spo + j
        return jnp.where(s < set_count, r.lens[jnp.minimum(s, set_count - 1)], 0)

    lengths = [length_of(j) for j in range(spo)]
    point_row = iota((rs, D), 0) % WIN * parts + iota((rs, D), 0) // WIN
    point_lane = iota((1, rs), 1) % WIN * parts + iota((1, rs), 1) // WIN

    def lanes(g):
        return slice(g * gsz * rs, (g + 1) * gsz * rs)

    def by_head(full):
        out = full[HEADS - 1]
        for h in range(HEADS - 2, -1, -1):
            out = jnp.where(headlane == h, full[h], out)
        return out

    def heads(rows):
        return jnp.concatenate([jnp.where(headlane == h, rows, 0.0) for h in range(HEADS)], axis=0)

    def expand(rows):
        rep = jnp.concatenate([r.diag[...] * rows[s : s + 1] for s in range(rows.shape[0])], axis=0)
        high, low = split(rep)
        return nn(jnp.concatenate([high, low], axis=1), r.ones2[...])

    def compress(values):
        high, low = split(values)
        wide = nn(jnp.concatenate([high, low], axis=1), r.ones2[...])
        return jnp.sum(wide.reshape(-1, IND, D) * r.diag[...][None], axis=1)

    def blocks(rows):
        return jnp.concatenate([rows] * HEADS, axis=0) * r.bd[...]

    def wide_gain(j, n):
        return jnp.concatenate([r.gF[j]] * (n // D), axis=1)

    def sets_of(g):
        return range(g * gsz, (g + 1) * gsz)

    def phase1(g):
        for j in sets_of(g):
            rows = slice(j * rs, (j + 1) * rs)
            x = r.xr[j].reshape(rs, D)
            kv = nn(x, r.w01kv[...]).astype(BF16)
            v1 = kv[:, D:]
            r.v1s[rows, :] = v1
            scores = nt(kv[:, 0:D], r.qB[...])
            inside = point_row < lengths[j]
            m = jnp.max(jnp.where(inside, scores, NEG), axis=0, keepdims=True)
            t = jnp.where(inside, scores - m, NEG)
            r.t1s[rows, :] = t
            p = jnp.exp(t)
            r.den1[j : j + 1, :] = jnp.sum(p, axis=0, keepdims=True)
            r.num1[j * IND : (j + 1) * IND, :] = by_head(tn(p.astype(BF16), v1).reshape(HEADS, IND, D))
            xt = x.T
            r.xT[:, rows] = xt
            r.q2T[:, rows] = (nn(r.w10T[...], xt) * FACTOR).astype(BF16)

    def ind_rows(g):
        return slice(g * gsz * IND, (g + 1) * gsz * IND)

    def phase2(g):
        at = ind_rows(g)
        rdx = expand(1.0 / jnp.maximum(r.den1[g * gsz : (g + 1) * gsz], 0.5))
        r.rdenx[at] = rdx
        att = r.num1[at] * rdx
        r.att1[at] = att
        query = jnp.concatenate([ind32] * gsz, axis=0)
        xh, sc = norm(query + nn(att.astype(BF16), r.outw[0]), 1)
        r.own0[0, at] = xh
        r.own0r[0, at] = sc
        h1 = xh * gains[0, 0][None, :]
        pre = nn(h1.astype(BF16), r.ff[0, 0])
        r.own0[1, at] = pre
        xh, sc = norm(h1 + nn(gelu(pre).astype(BF16), r.ff[0, 1]), 1)
        r.own0[2, at] = xh
        r.own0r[1, at] = sc
        k2 = (xh * gains[0, 1][None, :]).astype(BF16)
        r.k2s[at] = k2
        r.kv2s[at] = nn(k2, r.w1kv[...]).astype(BF16)

    def phase3(g):
        at = lanes(g)
        n = gsz * rs
        atts = []
        for j in sets_of(g):
            sl = slice(j * rs, (j + 1) * rs)
            kv2 = r.kv2s[j * IND : (j + 1) * IND]
            s = nn(blocks(kv2[:, 0:D]), r.q2T[:, sl]).reshape(HEADS, IND, rs)
            t = s - jnp.max(s, axis=1, keepdims=True)
            r.t2s[:, sl] = t.reshape(D, rs)
            p = jnp.exp(t)
            rden = 1.0 / jnp.sum(p, axis=1, keepdims=True)
            r.rden2s[:, :, sl] = rden
            num = tn(blocks(kv2[:, D:]), p.reshape(D, rs).astype(BF16))
            att = (num.reshape(HEADS, HD, rs) * rden).reshape(D, rs)
            r.attT[:, sl] = att
            atts.append(att)
        att = jnp.concatenate(atts, axis=1)
        xh, sc = norm(r.xT[:, at].astype(F32) + nn(r.tailT[0], att.astype(BF16)), 0)
        r.xh1s[:, at] = xh
        r.r1s[:, at] = sc
        h1 = xh * wide_gain(0, n)
        pre = nn(r.tailT[1], h1.astype(BF16))
        r.ps[:, at] = pre
        xh, sc = norm(h1 + nn(r.tailT[2], gelu(pre).astype(BF16)), 0)
        r.xh2s[:, at] = xh
        r.r2s[:, at] = sc
        m2 = (xh * wide_gain(1, n)).astype(BF16)
        r.m2b[:, at] = m2
        kv3 = nn(r.w2kvT[...], m2).astype(BF16)
        r.kv3T[:, at] = kv3
        s3 = nn(r.q3B[...], kv3[0:D])
        for i, j in enumerate(sets_of(g)):
            sl = slice(i * rs, (i + 1) * rs)
            inside = point_lane < lengths[j]
            m = jnp.max(jnp.where(inside, s3[:, sl], NEG), axis=1, keepdims=True)
            t = jnp.where(inside, s3[:, sl] - m, NEG)
            r.t3s[:, j * rs : (j + 1) * rs] = t
            p = jnp.exp(t)
            r.rden3[j * HS : (j + 1) * HS] = 1.0 / jnp.maximum(jnp.sum(p, axis=1, keepdims=True), 0.5)
            full = nt(p.astype(BF16), kv3[D:, sl])
            r.num3[j * SP : (j + 1) * SP] = by_head(full.reshape(HEADS, SP, D))

    g20, g21 = gains[2, 0][None, :], gains[2, 1][None, :]

    def phase4(g):
        rows3 = slice(g * gsz * SP, (g + 1) * gsz * SP)
        rden = r.rden3[g * gsz * HS : (g + 1) * gsz * HS]
        wide = jnp.broadcast_to(rden, (gsz * HS, D)).reshape(gsz, HEADS, SP, D)
        rdx = jnp.concatenate([by_head(wide[i]) for i in range(gsz)], axis=0)
        att = r.num3[rows3] * rdx
        attb = att.astype(BF16)
        query = jnp.concatenate([seed8] * gsz, axis=0)
        xha, ra = norm(query + nn(attb, r.outw[2]), 1)
        h1 = xha * g20
        h1b = h1.astype(BF16)
        pre = nn(h1b, r.ff[2, 0])
        act, dact = gelu_both(pre)
        actb = act.astype(BF16)
        xhb, rb = norm(h1 + nn(actb, r.ff[2, 1]), 1)
        pooled = xhb * g21
        cots = []
        for i, j in enumerate(sets_of(g)):
            s = me * spo + j
            cot = r.cot[jnp.minimum(s, set_count - 1)].astype(F32)
            cots += [jnp.where(s < set_count, cot, 0.0), jnp.zeros((SP - SEEDS, D), F32)]
            r.poolrow[j * SEEDS : (j + 1) * SEEDS] = pooled[i * SP : i * SP + SEEDS]
        d_out = jnp.concatenate(cots, axis=0)
        d_b = norm_back(d_out, g21, xhb, rb, 1)
        d_bb = d_b.astype(BF16)
        d_pre = (dact * nt(d_bb, r.ff[2, 1])).astype(BF16)
        d_h1 = d_b + nt(d_pre, r.ff[2, 0])
        d_c = norm_back(d_h1, g20, xha, ra, 1)
        d_cb = d_c.astype(BF16)
        d_att = nt(d_cb, r.outw[2])
        dn = (d_att * rdx).astype(BF16).astype(F32)
        prod = d_att * att
        for i, j in enumerate(sets_of(g)):
            at = slice(j * HS, (j + 1) * HS)
            r.d3s[at] = heads(dn[i * SP : (i + 1) * SP]).astype(BF16)
            sums = jnp.sum(heads(prod[i * SP : (i + 1) * SP]), axis=1, keepdims=True)
            r.dd3[at] = -sums * rden[i * HS : (i + 1) * HS]
        r.s0[8 * D : 9 * D] += tn(attb, d_cb)
        r.s0[9 * D : 10 * D] += tn(h1b, d_pre)
        r.s0[10 * D : 11 * D] += tn(actb, d_bb)
        r.s0[11 * D + 8 : 11 * D + 16] += jnp.sum(d_c.reshape(gsz, SP, D), axis=0)
        r.s0[11 * D + 24 : 11 * D + 25] += jnp.sum(d_h1 * xha, axis=0, keepdims=True)
        r.s0[11 * D + 25 : 11 * D + 26] += jnp.sum(d_out * xhb, axis=0, keepdims=True)

    def fold(values):
        return total([values[:, k * D : (k + 1) * D] for k in range(values.shape[1] // D)])

    def phase5(g):
        at = lanes(g)
        n = gsz * rs
        kv3 = r.kv3T[:, at]
        ds3s, dv3s = [], []
        for i, j in enumerate(sets_of(g)):
            sl = slice(i * rs, (i + 1) * rs)
            d3 = r.d3s[j * HS : (j + 1) * HS]
            t = r.t3s[:, j * rs : (j + 1) * rs]
            p = jnp.exp(t)
            e = p * (nn(d3, kv3[D:, sl]) + r.dd3[j * HS : (j + 1) * HS])
            ds3s.append((e - jnp.where(t == 0.0, jnp.sum(e, axis=1, keepdims=True), 0.0)).astype(BF16))
            dv3s.append(tn(d3, p.astype(BF16)))
        ds3 = jnp.concatenate(ds3s, axis=1)
        dk3 = nn(r.q3BT[:, 0:HS], ds3)
        dkv3 = jnp.concatenate([dk3, jnp.concatenate(dv3s, axis=1)], axis=0).astype(BF16)
        r.dq3[...] += nt(ds3, kv3[0:D])
        dw = nt(r.m2b[:, at], dkv3)
        r.s0[3 * D : 4 * D] += dw[:, 0:D]
        r.s0[4 * D : 5 * D] += dw[:, D:]
        d_m = nn(r.w2kv[...], dkv3)
        xh2 = r.xh2s[:, at]
        r.gacc[1] += fold(d_m * xh2)
        d_b = norm_back(d_m, wide_gain(1, n), xh2, r.r2s[:, at], 0)
        d_bb = d_b.astype(BF16)
        act, dact = gelu_both(r.ps[:, at])
        r.s0[7 * D : 8 * D] += nt(act.astype(BF16), d_bb)
        d_pre = (dact * nn(r.ff[1, 1], d_bb)).astype(BF16)
        xh1 = r.xh1s[:, at]
        g0 = wide_gain(0, n)
        r.s0[6 * D : 7 * D] += nt((xh1 * g0).astype(BF16), d_pre)
        d_h1 = d_b + nn(r.ff[1, 0], d_pre)
        r.gacc[0] += fold(d_h1 * xh1)
        d_c = norm_back(d_h1, g0, xh1, r.r1s[:, at], 0)
        d_cb = d_c.astype(BF16)
        att = r.attT[:, at]
        r.s0[5 * D : 6 * D] += nt(att.astype(BF16), d_cb)
        d_att = nn(r.outw[1], d_cb)
        rden = r.rden2s[:, :, at]
        d_num = (d_att.reshape(HEADS, HD, n) * rden).reshape(D, n).astype(BF16)
        dden = -jnp.sum((d_att * att).reshape(HEADS, HD, n), axis=1, keepdims=True) * rden
        dqs, dks, dvs = [], [], []
        for i, j in enumerate(sets_of(g)):
            sl = slice(i * rs, (i + 1) * rs)
            own = slice(j * rs, (j + 1) * rs)
            kv2 = r.kv2s[j * IND : (j + 1) * IND]
            dp = nn(blocks(kv2[:, D:]), d_num[:, sl]).reshape(HEADS, IND, rs)
            t = r.t2s[:, own].reshape(HEADS, IND, rs)
            p = jnp.exp(t)
            e = p * (dp + dden[:, :, sl])
            ds = (e - jnp.where(t == 0.0, jnp.sum(e, axis=1, keepdims=True), 0.0)).reshape(D, rs).astype(BF16)
            dqs.append(tn(blocks(kv2[:, 0:D]), ds))
            dks.append(by_head(nt(ds, r.q2T[:, own]).reshape(HEADS, IND, D)))
            dvs.append(by_head(nt(p.reshape(D, rs).astype(BF16), d_num[:, sl]).reshape(HEADS, IND, D)))
        dq = (jnp.concatenate(dqs, axis=1) * FACTOR).astype(BF16)
        r.s0[0:D] += nt(r.xT[:, at], dq)
        r.dxT[:, at] = d_c + nn(r.proj[1, 0], dq)
        dkv2 = jnp.concatenate([jnp.concatenate(dks, axis=0), jnp.concatenate(dvs, axis=0)], axis=1).astype(BF16)
        rows = ind_rows(g)
        r.dk2s[rows] = nt(dkv2, r.w1kv[...])
        dw = tn(r.k2s[rows], dkv2)
        r.s0[D : 2 * D] += dw[:, 0:D]
        r.s0[2 * D : 3 * D] += dw[:, D:]

    g00, g01 = gains[0, 0][None, :], gains[0, 1][None, :]

    def phase6(g):
        at = ind_rows(g)
        d_out = r.dk2s[at]
        xha, pre, xhb = r.own0[0, at], r.own0[1, at], r.own0[2, at]
        d_b = norm_back(d_out, g01, xhb, r.own0r[1, at], 1)
        d_bb = d_b.astype(BF16)
        act, dact = gelu_both(pre)
        d_pre = (dact * nt(d_bb, r.ff[0, 1])).astype(BF16)
        d_h1 = d_b + nt(d_pre, r.ff[0, 0])
        d_c = norm_back(d_h1, g00, xha, r.own0r[0, at], 1)
        d_cb = d_c.astype(BF16)
        d_att = nt(d_cb, r.outw[0])
        att = r.att1[at]
        r.dn1[at] = (d_att * r.rdenx[at]).astype(BF16)
        sets = slice(g * gsz, (g + 1) * gsz)
        r.dden1[sets] = -compress(d_att * att) / jnp.maximum(r.den1[sets], 0.5)
        r.s1[0:D] += tn(att.astype(BF16), d_cb)
        r.s1[D : 2 * D] += tn((xha * g00).astype(BF16), d_pre)
        r.s1[2 * D : 3 * D] += tn(act.astype(BF16), d_bb)
        r.s1[5 * D : 5 * D + IND] += jnp.sum(d_c.reshape(gsz, IND, D), axis=0)
        r.s1[5 * D + IND : 5 * D + IND + 1] += jnp.sum(d_h1 * xha, axis=0, keepdims=True)
        r.s1[5 * D + IND + 1 : 5 * D + IND + 2] += jnp.sum(d_out * xhb, axis=0, keepdims=True)

    def phase7(g):
        for j in sets_of(g):
            rows = slice(j * rs, (j + 1) * rs)
            db = blocks(r.dn1[j * IND : (j + 1) * IND])
            t = r.t1s[rows, :]
            p = jnp.exp(t)
            e = p * (nt(r.v1s[rows, :], db) + r.dden1[j : j + 1])
            ds = (e - jnp.where(t == 0.0, jnp.sum(e, axis=0, keepdims=True), 0.0)).astype(BF16)
            dv = nn(p.astype(BF16), db).astype(BF16)
            dsdv = jnp.concatenate([ds, dv], axis=1)
            dw = nn(r.xT[:, rows], dsdv)
            r.s1[3 * D : 4 * D] += dw[:, 0:D]
            r.s1[4 * D : 5 * D] += dw[:, D:]
            r.pgs[j] = (nn(dsdv, r.gW[...]) + r.dxT[:, rows].T).astype(BF16).reshape(parts, WIN, D)

    def send_back(g):
        for j in sets_of(g):
            r.pgr[j, me] = r.pgs[j, me]
            exchange(("pg", j), "pts", spo + j, lambda dev: r.pgs.at[j, dev], lambda dev: r.pgr.at[j, dev])

    slabs = [tuple(getattr(r, f"s{k}{x}") for x in ("", "b", "r", "h", "g")) for k in range(len(SLABS))]

    def slab_start(which):
        f_ref, b_ref, r_ref, _, _ = slabs[which]
        b_ref[...] = f_ref[...].reshape(b_ref.shape).astype(BF16)
        exchange(("rs", which), "layer", which, lambda dev: b_ref.at[dev], lambda dev: r_ref.at[dev])
        r_ref[q] = b_ref[q]

    def slab_mid(which):
        _, _, r_ref, h_ref, _ = slabs[which]
        arrive(("rs", which))
        h_ref[hi] = total([r_ref[j].astype(F32) for j in range(qn)]).astype(BF16)
        exchange(("z", which), "column", which, lambda dev: h_ref.at[hi], lambda dev: h_ref.at[dev])

    def slab_gather(which):
        _, _, _, h_ref, g_ref = slabs[which]
        arrive(("z", which))
        g_ref[q] = total([h_ref[j].astype(F32) for j in range(hn)]).astype(BF16)
        exchange(("ag", which), "layer", len(SLABS) + which, lambda dev: g_ref.at[q], lambda dev: g_ref.at[dev])

    def slab_finish(which):
        arrive(("ag", which))
        return slabs[which][4][...].reshape(-1, D)

    def take(g):
        for j in sets_of(g):
            arrive(("x", j))

    for g in range(ng):
        take(g)
        phase1(g)
        phase2(g)
        phase3(g)
        phase4(g)
    exchange("pool", "pts", 2 * spo, lambda dev: r.poolrow, lambda dev: r.poolall.at[dev])
    r.poolall[me] = r.poolrow[...]
    for g in range(ng):
        phase5(g)
        if g == ng - 1:
            r.s0[11 * D : 11 * D + 8] = by_head(r.dq3[...].reshape(HEADS, SP, D))
            for j in range(2):
                r.s0[11 * D + 16 + j : 11 * D + 17 + j] = jnp.sum(r.gacc[j].T, axis=0, keepdims=True)
            slab_start(0)
        phase6(g)
        phase7(g)
        send_back(g)
    slab_start(1)
    slab_mid(0)
    slab_mid(1)
    slab_gather(0)

    for j in range(spo):
        arrive(("pg", j))
    for s in range(SLOTS):
        r.pgpad[s * WIN : (s + 1) * WIN, :] = r.pgr[s % spo, s // spo].astype(F32)
    sub8 = iota((8, D), 0)

    def unpad(t, a):
        def half(at, a):
            b = jnp.minimum(a + 1, SLOTS - 1)
            end = r.starts[b]
            first = r.pgpad[pl.ds(jnp.minimum(a * WIN + at - r.starts[a], ROWS - 8), 8), :]
            second = r.pgpad[pl.ds(jnp.minimum(b * WIN + at - end, ROWS - 8), 8), :]
            return jnp.where(at + sub8 < end, first, second), jnp.where((end <= at + 8) & (a < SLOTS - 1), a + 1, a)

        upper, a = half(t * 16, a)
        lower, a = half(t * 16 + 8, a)
        r.pg_o[pl.ds(pl.multiple_of(t * 16, 16), 16), :] = jnp.concatenate([upper, lower], axis=0).astype(BF16)
        return a

    lax.fori_loop(0, ROWS // 16, unpad, jnp.int32(0))

    slab_gather(1)

    slab = slab_finish(0)
    mats = [slab[k * D : (k + 1) * D].astype(F32) for k in range(SLABS[0])]
    for k, place in enumerate(((1, 0), (1, 1), (1, 2), (2, 1), (2, 2))):
        r.projg_o[place] = mats[k]
    r.outg_o[1] = mats[5]
    r.ffg_o[1, 0] = mats[6]
    r.ffg_o[1, 1] = mats[7]
    r.outg_o[2] = mats[8]
    r.ffg_o[2, 0] = mats[9]
    r.ffg_o[2, 1] = mats[10]
    misc = mats[11]
    r.gaing_o[1] = misc[16:18]
    r.gaing_o[2] = misc[24:26]
    dq3 = jnp.concatenate([misc[0:SEEDS] * FACTOR, jnp.zeros((16 - SEEDS, D), F32)], axis=0)
    high, low = split(dq3)
    r.seedg_o[...] = (nt(high, r.proj[2, 0]) + nt(low, r.proj[2, 0]))[0:SEEDS] + misc[8 : 8 + SEEDS]
    r.projg_o[2, 0] = tn(seed16, high) + tn(seed16, low)
    arrive("pool")
    for s in range(set_count):
        j = s % spo
        r.pool_o[s] = r.poolall[s // spo, j * SEEDS : (j + 1) * SEEDS].astype(BF16)

    slab = slab_finish(1)
    r.outg_o[0] = slab[0:D].astype(F32)
    r.ffg_o[0, 0] = slab[D : 2 * D].astype(F32)
    r.ffg_o[0, 1] = slab[2 * D : 3 * D].astype(F32)
    r.projg_o[0, 2] = slab[4 * D : 5 * D].astype(F32)
    misc = slab[5 * D : 6 * D].astype(F32)
    r.gaing_o[0] = misc[IND : IND + 2]
    tsum = slab[3 * D : 4 * D]
    r.projg_o[0, 1] = nn(tsum, r.qB[...])
    dq1 = by_head(tn(tsum, r.proj[0, 1]).reshape(HEADS, IND, D)) * FACTOR
    high, low = split(dq1)
    r.indg_o[...] = misc[0:IND] + nt(high, r.proj[0, 0]) + nt(low, r.proj[0, 0])
    r.projg_o[0, 0] = tn(r.ind[...], high) + tn(r.ind[...], low)
    flush()


def write_out(*refs):
    n = len(OUT_NAMES)
    sems = refs[2 * n]
    copies = [pltpu.make_async_copy(refs[j], refs[n + j], sems.at[j]) for j in range(n)]
    for c in copies:
        c.start()
    for c in copies:
        c.wait()


def local(parts, groups, points, set_lengths, projections, outputs, feedforward, gains, inducing, seeds, cotangent):
    set_count = set_lengths.shape[0]
    cfg = plan(parts, groups)
    args = (set_lengths, points, projections, outputs, feedforward, gains, inducing, seeds, cotangent)
    table = {}
    for name, a in zip(IN_NAMES, args):
        table[name] = pltpu.SMEM(a.shape, a.dtype) if name == "lens" else pltpu.VMEM(a.shape, a.dtype)
    table.update(scratch_table(cfg))
    vmem = pl.BlockSpec(memory_space=pltpu.VMEM)
    hbm = pl.BlockSpec(memory_space=pltpu.HBM)
    args = tuple(pltpu.with_memory_space_constraint(a, pltpu.HBM) for a in args)
    out_shape = [
        jax.ShapeDtypeStruct((set_count, SEEDS, D), BF16),
        jax.ShapeDtypeStruct(points.shape, BF16),
        jax.ShapeDtypeStruct((3, 3, D, D), F32),
        jax.ShapeDtypeStruct((3, D, D), F32),
        jax.ShapeDtypeStruct((3, 2, D, D), F32),
        jax.ShapeDtypeStruct((3, 2, D), F32),
        jax.ShapeDtypeStruct((IND, D), F32),
        jax.ShapeDtypeStruct((SEEDS, D), F32),
    ]
    n = len(out_shape)
    results = pl.pallas_call(
        functools.partial(kernel, cfg, set_count, tuple(table)),
        out_shape=[pltpu.VMEM(o.shape, o.dtype) for o in out_shape],
        in_specs=[hbm] * len(args),
        out_specs=[vmem] * n,
        scratch_shapes=list(table.values()),
        compiler_params=pltpu.CompilerParams(
            collective_id=0, has_side_effects=True, vmem_limit_bytes=48 * 1024 * 1024
        ),
    )(*args)
    results = [pltpu.with_memory_space_constraint(a, pltpu.VMEM) for a in results]
    return tuple(
        pl.pallas_call(
            write_out,
            out_shape=out_shape,
            in_specs=[vmem] * n,
            out_specs=[hbm] * n,
            scratch_shapes=[pltpu.SemaphoreType.DMA((n,))],
        )(*results)
    )


def solution(mesh):
    parts, groups = mesh.shape["pts"], mesh.shape["sets"]
    placed = (P(("sets", "pts"), None), P("sets"), P(), P(), P(), P(), P(), P(), P("sets", None, None))
    return jax.shard_map(
        functools.partial(local, parts, groups),
        mesh=mesh,
        in_specs=placed,
        out_specs=(P("sets", None, None), P(("sets", "pts"), None), P(), P(), P(), P(), P(), P()),
        check_vma=False,
    )
```

```python
import functools
import math
import types

import jax
import jax.numpy as jnp
from jax import lax
from jax.experimental import pallas as pl
from jax.experimental.pallas import tpu as pltpu
from jax.sharding import PartitionSpec as P

MESH = pl.DeviceIdType.MESH
F32 = jnp.float32
BF16 = jnp.bfloat16
D = 128
HEADS = 4
HD = 32
IND = 32
SEEDS = 4
SP = 8
HS = HEADS * SP
SLOTS = 32
WIN = 64
ROWS = SLOTS * WIN
NEG = -1e30
FACTOR = HD**-0.5
G0 = math.sqrt(2.0 / math.pi)
G1 = 0.044715
SLABS = (
    (("O2", "U2", "E2", "W22"), True),
    (("E1", "U1", "O1", "W10", "W11", "W12"), True),
    (("O0", "U0", "E0", "misc", "T", "W02"), False),
)
WHERE = {name: (k, at * D) for k, (mats, _) in enumerate(SLABS) for at, name in enumerate(mats)}
T3, DSEED, GAIN, DIND = 0, 32, 40, 48
LB = 128
STAGES = 45
PLAN = ({0: 16}, {0: 28, 1: 12}, {0: 45, 1: 22, 2: 8}, {1: 45, 2: 18, 3: 18}, {2: 45, 3: 38})


def nn(a, b):
    return lax.dot_general(a, b, (((1,), (0,)), ((), ())), preferred_element_type=F32)


def nt(a, b):
    return lax.dot_general(a, b, (((1,), (1,)), ((), ())), preferred_element_type=F32)


def tn(a, b):
    return lax.dot_general(a, b, (((0,), (0,)), ((), ())), preferred_element_type=F32)


def split(x):
    high = x.astype(BF16)
    return high, (x - high.astype(F32)).astype(BF16)


def iota(shape, dim):
    return lax.broadcasted_iota(jnp.int32, shape, dim)


def total(values):
    return functools.reduce(jnp.add, values)


def norm(values, axis):
    center = values - jnp.mean(values, axis=axis, keepdims=True)
    scale = lax.rsqrt(jnp.mean(center * center, axis=axis, keepdims=True) + 1e-05)
    return center * scale, scale


def norm_back(d_out, gain, hat, scale, axis):
    scaled = d_out * gain
    first = jnp.mean(scaled, axis=axis, keepdims=True)
    second = jnp.mean(scaled * hat, axis=axis, keepdims=True)
    return scale * (scaled - first - hat * second)


def gelu(v):
    th = jnp.tanh(G0 * (v + G1 * (v * v * v)))
    return 0.5 * v * (1.0 + th)


def gelu_both(v):
    sq = v * v
    th = jnp.tanh(v * (G0 + (G0 * G1) * sq))
    half = 0.5 + 0.5 * th
    return v * half, half + (0.5 * v) * (1.0 - th * th) * (G0 + (3.0 * G0 * G1) * sq)


def plan(parts, groups):
    spo = SLOTS // parts
    return types.SimpleNamespace(
        parts=parts, groups=groups, spo=spo, rs=parts * WIN, qn=2 * groups, hn=parts // 2, pool=max(8, spo * SEEDS),
    )


def slab_rows(mats, cfg):
    unit = 16 * cfg.qn
    return (mats * D + unit - 1) // unit * unit


def scratch_table(cfg):
    table = {}

    def vm(name, shape, kind=F32):
        table[name] = pltpu.VMEM(shape, kind)

    spo, parts = cfg.spo, cfg.parts
    table["starts"] = pltpu.SMEM((SLOTS,), jnp.int32)
    for name in ("first", "second", "edge"):
        table[name] = pltpu.SMEM((ROWS // 8,), jnp.int32)
    vm("pf32", (ROWS, D))
    vm("xs", (spo, parts, WIN, D), BF16)
    vm("xr", (spo, parts, WIN, D), BF16)
    vm("pgs", (spo, parts, WIN, D), BF16)
    vm("pgr", (spo, parts, WIN, D), BF16)
    vm("pgpad", (ROWS, D))
    vm("v1s", (ROWS, D), BF16)
    vm("t1s", (ROWS, D))
    for name in ("t2s", "attT", "xh1s", "dacts", "xh2s", "dxT"):
        vm(name, (D, ROWS))
    for name in ("xT", "q2T", "m2b", "actb"):
        vm(name, (D, ROWS), BF16)
    vm("v3T", (D, ROWS), BF16)
    vm("t3s", (HS, ROWS))
    vm("rden2s", (HEADS, 1, ROWS))
    vm("r1s", (1, ROWS))
    vm("r2s", (1, ROWS))
    vm("k2s", (spo * IND, D), BF16)
    vm("kv2s", (spo * IND, 2 * D), BF16)
    vm("num1", (spo * IND, D))
    vm("den1", (spo, D))
    vm("att1", (spo * IND, D))
    vm("rdenx", (spo * IND, D))
    vm("own0", (3, spo * IND, D))
    vm("own0r", (2, spo * IND, 1))
    vm("dk2s", (spo * IND, D))
    vm("dn1", (spo * IND, D), BF16)
    vm("dden1", (spo, D))
    vm("num3", (spo * SP, D))
    vm("rden3", (spo * HS, 1))
    vm("d3s", (spo * HS, D), BF16)
    vm("dd3", (spo * HS, 1))
    vm("poolrow", (cfg.pool, D))
    vm("poolall", (parts, cfg.pool, D))
    vm("bd", (D, D), BF16)
    vm("ones2", (2 * D, D), BF16)
    vm("diag", (IND, D))
    vm("gF", (2, D, D))
    vm("w01", (D, 2 * D), BF16)
    vm("w01T", (2 * D, D), BF16)
    vm("w1kv", (D, 2 * D), BF16)
    vm("w2kvT", (2 * D, D), BF16)
    vm("w2d", (D, 2 * D), BF16)
    vm("w10T", (D, D), BF16)
    vm("tailT", (3, D, D), BF16)
    vm("qB", (D, D), BF16)
    vm("q3B", (HS, D), BF16)
    vm("gacc", (2, D, D))
    for k, (mats, by_core) in enumerate(SLABS):
        rows = slab_rows(len(mats), cfg)
        part = rows // cfg.qn
        vm(f"s{k}", (rows, D))
        vm(f"s{k}b", (cfg.qn, part, D), BF16)
        vm(f"s{k}g", (cfg.qn, part, D), BF16)
        vm(f"s{k}h", (cfg.hn, part, D), BF16)
        if by_core:
            vm(f"s{k}c", (cfg.groups, part, D), BF16)
            vm(f"s{k}x", (cfg.groups, part, D), BF16)
        vm(f"s{k}r", (cfg.groups if by_core else cfg.qn, part, D), BF16)
    table["in_sem"] = pltpu.SemaphoreType.DMA((9,))
    for name in ("ssem", "rsem"):
        table[name] = pltpu.SemaphoreType.DMA((2 * spo + 1, parts))
    for line, count in (("layer", cfg.qn), ("flat", cfg.groups), ("column", cfg.hn), ("core", 2)):
        for way in ("s", "r"):
            table[line + way] = pltpu.SemaphoreType.DMA((2 * len(SLABS), count))
    return table


IN_NAMES = ("lens", "pts", "proj", "outw", "ff", "gain", "ind", "seed", "cot")
OUT_NAMES = ("pool_o", "pg_o", "projg_o", "outg_o", "ffg_o", "gaing_o", "indg_o", "seedg_o")


def kernel(cfg, set_count, names, *refs):
    n_in, n_out = len(IN_NAMES), len(OUT_NAMES)
    hbm = dict(zip(IN_NAMES, refs[:n_in]))
    r = types.SimpleNamespace(**dict(zip(OUT_NAMES, refs[n_in : n_in + n_out])), **dict(zip(names, refs[n_in + n_out :])))
    parts, groups, spo, rs, qn, hn = cfg.parts, cfg.groups, cfg.spo, cfg.rs, cfg.qn, cfg.hn
    me = lax.axis_index("pts")
    mine = lax.axis_index("sets")
    lo, hi = lax.rem(me, 2), lax.div(me, 2)
    core = lax.rem(mine, 2)
    flat = mine - core + lo
    q = lo * groups + mine

    barrier = pltpu.get_barrier_semaphore()
    for k in range(1, parts):
        pl.semaphore_signal(barrier, inc=1, device_id={"pts": lax.rem(me + k, parts)}, device_id_type=MESH)
    for k in range(1, groups):
        for j in range(2):
            at = {"sets": lax.rem(mine + k, groups), "pts": hi * 2 + j}
            pl.semaphore_signal(barrier, inc=1, device_id=at, device_id_type=MESH)
    peers = parts - 1 + 2 * (groups - 1)

    loads = {
        name: pltpu.make_async_copy(hbm[name], getattr(r, name), r.in_sem.at[j]) for j, name in enumerate(IN_NAMES)
    }
    for name in IN_NAMES:
        loads[name].start()

    leaving, coming = [], {}
    lines = {
        "pts": (parts, me, r.ssem, r.rsem, lambda dev: {"pts": dev}),
        "layer": (qn, q, r.layers, r.layerr, lambda dev: {"sets": lax.rem(dev, groups), "pts": hi * 2 + lax.div(dev, groups)}),
        "flat": (
            groups, flat, r.flats, r.flatr,
            lambda dev: {"sets": lax.div(dev, 2) * 2 + core, "pts": hi * 2 + lax.rem(dev, 2)},
        ),
        "column": (hn, hi, r.columns, r.columnr, lambda dev: {"pts": dev * 2 + lo}),
        "core": (2, core, r.cores, r.corer, lambda dev: {"sets": mine - core + dev}),
    }

    def exchange(key, line, index, source, land):
        count, own, send_sem, recv_sem, where = lines[line]
        waits = coming.setdefault(key, [])
        for k in range(1, count):
            dev = lax.rem(own + k, count)
            sent = pltpu.make_async_remote_copy(
                src_ref=source(dev), dst_ref=land(own), send_sem=send_sem.at[index, dev],
                recv_sem=recv_sem.at[index, own], device_id=where(dev), device_id_type=MESH,
            )
            sent.start()
            leaving.append((key, sent))
            waits.append(
                pltpu.make_async_remote_copy(
                    src_ref=land(dev), dst_ref=land(dev), send_sem=send_sem.at[index, dev],
                    recv_sem=recv_sem.at[index, dev], device_id=where(dev), device_id_type=MESH,
                )
            )

    def arrive(key):
        for wait in coming.pop(key):
            wait.wait_recv()

    def drain(*keys):
        for item in list(leaving):
            if not keys or item[0] in keys:
                item[1].wait_send()
                leaving.remove(item)

    def flush():
        for key in list(coming):
            arrive(key)
        drain()

    loads["lens"].wait()

    def table(s, start):
        length = r.lens[jnp.minimum(s, set_count - 1)]
        r.starts[s] = start
        return start + jnp.where(s < set_count, lax.div(length - me + parts - 1, parts), 0)

    lax.fori_loop(0, SLOTS, table, jnp.int32(0))
    loads["pts"].wait()
    r.pf32[...] = r.pts[...].astype(F32)

    def gather(j):
        for o in range(parts):
            r.xs[j, o] = r.pf32[pl.ds(r.starts[o * spo + j], WIN), :].astype(BF16)
        r.xr[j, me] = r.xs[j, me]

    gather(0)
    pl.semaphore_wait(barrier, peers)
    for j in range(spo):
        if j:
            gather(j)
        exchange(("x", j), "pts", j, lambda dev: r.xs.at[j, dev], lambda dev: r.xr.at[j, dev])

    row128 = iota((D, D), 0)
    lane128 = iota((D, D), 1)
    headlane = iota((1, D), 1) // HD
    bdv = jnp.where((row128 // HD) == (lane128 // HD), 1.0, 0.0).astype(BF16)
    r.bd[...] = bdv
    r.ones2[0:D, :] = bdv
    r.ones2[D:, :] = bdv
    r.diag[...] = jnp.where((iota((IND, D), 1) % HD) == iota((IND, D), 0), 1.0, 0.0)
    for name in IN_NAMES[2:]:
        loads[name].wait()
    r.w1kv[:, 0:D] = r.proj[1, 1]
    r.w1kv[:, D:] = r.proj[1, 2]
    r.w10T[...] = r.proj[1, 0].T
    r.w2kvT[0:D, :] = r.proj[2, 1].T
    r.w2kvT[D:, :] = r.proj[2, 2].T
    r.tailT[0] = r.outw[1].T
    r.tailT[1] = r.ff[1, 0].T
    r.tailT[2] = r.ff[1, 1].T
    gains = r.gain[...].astype(F32)
    for j in range(2):
        r.gF[j] = jnp.broadcast_to(gains[1, j][None, :], (D, D)).T
    q1 = (nn(r.ind[...], r.proj[0, 0]) * FACTOR).astype(BF16)
    r.qB[...] = jnp.concatenate([q1] * HEADS, axis=0) * bdv
    r.w01[:, 0:D] = r.proj[0, 1]
    r.w01[:, D:] = r.proj[0, 2]
    r.w01T[0:D, :] = nt(r.qB[...], r.proj[0, 1]).astype(BF16)
    r.w01T[D:, :] = r.proj[0, 2].T
    ind32 = r.ind[...].astype(F32)
    seed8 = jnp.concatenate([r.seed[...].astype(F32), jnp.zeros((SP - SEEDS, D), F32)], axis=0)
    seed16 = jnp.concatenate([seed8, jnp.zeros((SP, D), F32)], axis=0).astype(BF16)
    q3 = (nn(seed16, r.proj[2, 0]) * FACTOR).astype(BF16).astype(F32)[0:SP]
    q3f = jnp.concatenate([jnp.where(headlane == h, q3, 0.0) for h in range(HEADS)], axis=0)
    r.q3B[...] = q3f.astype(BF16)
    f3 = nt(r.q3B[...], r.proj[2, 1])
    r.w2d[:, 0:D] = jnp.concatenate([f3, jnp.zeros((D - HS, D), F32)], axis=0).T.astype(BF16)
    r.w2d[:, D:] = r.proj[2, 2]
    for s in (r.gacc, r.poolrow, *(getattr(r, f"s{k}") for k in range(len(SLABS)))):
        s[...] = jnp.zeros_like(s)

    def rows_of(t, a):
        at = t * 8
        b = jnp.minimum(a + 1, SLOTS - 1)
        end = r.starts[b]
        r.first[t] = jnp.minimum(a * WIN + at - r.starts[a], ROWS - 8)
        r.second[t] = jnp.minimum(b * WIN + at - end, ROWS - 8)
        r.edge[t] = end - at
        return jnp.where((end <= at + 8) & (a < SLOTS - 1), a + 1, a)

    lax.fori_loop(0, ROWS // 8, rows_of, jnp.int32(0))

    def length_of(j):
        s = me * spo + j
        return jnp.where(s < set_count, r.lens[jnp.minimum(s, set_count - 1)], 0)

    lengths = [length_of(j) for j in range(spo)]
    point_row = iota((rs, D), 0) % WIN * parts + iota((rs, D), 0) // WIN
    point_lane = iota((1, rs), 1) % WIN * parts + iota((1, rs), 1) // WIN

    def by_head(full):
        out = full[HEADS - 1]
        for h in range(HEADS - 2, -1, -1):
            out = jnp.where(headlane == h, full[h], out)
        return out

    def heads(rows):
        return jnp.concatenate([jnp.where(headlane == h, rows, 0.0) for h in range(HEADS)], axis=0)

    def expand(rows):
        rep = jnp.concatenate([r.diag[...] * rows[s : s + 1] for s in range(rows.shape[0])], axis=0)
        high, low = split(rep)
        return nn(jnp.concatenate([high, low], axis=1), r.ones2[...])

    def compress(values):
        high, low = split(values)
        wide = nn(jnp.concatenate([high, low], axis=1), r.ones2[...])
        return jnp.sum(wide.reshape(-1, IND, D) * r.diag[...][None], axis=1)

    def blocks(rows):
        return jnp.concatenate([rows] * HEADS, axis=0) * r.bd[...]

    def wide_gain(j):
        return r.gF[j] if LB == D else jnp.concatenate([r.gF[j]] * (LB // D), axis=1)

    def cut(j):
        return [slice(j * rs + b, j * rs + b + LB) for b in range(0, rs, LB)]

    def join(pieces, axis=1):
        return jnp.concatenate(pieces, axis=axis)

    slabs = [getattr(r, f"s{k}") for k in range(len(SLABS))]
    marks = {}

    def add(name, value, row=0):
        k, at = WHERE[name]
        slabs[k][at + row : at + row + value.shape[0]] += value
        marks[name, row] = marks.get((name, row), 0) + 1

    def lanes(j):
        return slice(j * rs, (j + 1) * rs)

    def ind_rows(j):
        return slice(j * IND, (j + 1) * IND)

    def phase1(j):
        at = lanes(j)
        x = r.xr[j].reshape(rs, D)
        both = [nn(x[b : b + LB], r.w01[...]).astype(BF16) for b in range(0, rs, LB)]
        for rows, v in zip(cut(j), both):
            r.v1s[rows, :] = v[:, D:]
        yield
        scores = [nt(v[:, 0:D], r.qB[...]) for v in both]
        r.xT[:, at] = x.T
        yield
        for sl in cut(j):
            r.q2T[:, sl] = (nn(r.w10T[...], r.xT[:, sl]) * FACTOR).astype(BF16)
        kept = [jnp.where(point_row[b : b + LB] < lengths[j], v, NEG) for b, v in zip(range(0, rs, LB), scores)]
        m = jnp.max(functools.reduce(jnp.maximum, kept), axis=0, keepdims=True)
        sums, ps = [], []
        for b, rows, v in zip(range(0, rs, LB), cut(j), scores):
            t = jnp.where(point_row[b : b + LB] < lengths[j], v - m, NEG)
            r.t1s[rows, :] = t
            p = jnp.exp(t)
            sums.append(p)
            ps.append(p.astype(BF16))
        full = tn(join(ps, 0), r.v1s[at, :]).reshape(HEADS, IND, D)
        yield
        r.den1[j : j + 1, :] = jnp.sum(total(sums), axis=0, keepdims=True)
        r.num1[ind_rows(j), :] = by_head(full)
        yield

    def phase2(j):
        at = ind_rows(j)
        rdx = expand(1.0 / jnp.maximum(r.den1[j : j + 1], 0.5))
        yield
        r.rdenx[at] = rdx
        att = r.num1[at] * rdx
        r.att1[at] = att
        xh, sc = norm(ind32 + nn(att.astype(BF16), r.outw[0]), 1)
        yield
        r.own0[0, at] = xh
        r.own0r[0, at] = sc
        h1 = xh * gains[0, 0][None, :]
        pre = nn(h1.astype(BF16), r.ff[0, 0])
        yield
        r.own0[1, at] = pre
        xh, sc = norm(h1 + nn(gelu(pre).astype(BF16), r.ff[0, 1]), 1)
        yield
        r.own0[2, at] = xh
        r.own0r[1, at] = sc
        k2 = (xh * gains[0, 1][None, :]).astype(BF16)
        r.k2s[at] = k2
        r.kv2s[at] = nn(k2, r.w1kv[...]).astype(BF16)
        yield

    def phase3(j):
        at = lanes(j)
        kv2 = r.kv2s[ind_rows(j)]
        kb, vb = blocks(kv2[:, 0:D]), blocks(kv2[:, D:])
        scores = [nn(kb, r.q2T[:, sl]).reshape(HEADS, IND, LB) for sl in cut(j)]
        yield
        nums, rdens = [], []
        for sl, s in zip(cut(j), scores):
            t = s - jnp.max(s, axis=1, keepdims=True)
            r.t2s[:, sl] = t.reshape(D, LB)
            p = jnp.exp(t)
            rden = 1.0 / jnp.sum(p, axis=1, keepdims=True)
            r.rden2s[:, :, sl] = rden
            rdens.append(rden)
            nums.append(tn(vb, p.reshape(D, LB).astype(BF16)))
        yield
        mixed = []
        for sl, num, rden in zip(cut(j), nums, rdens):
            att = (num.reshape(HEADS, HD, LB) * rden).reshape(D, LB)
            r.attT[:, sl] = att
            mixed.append(nn(r.tailT[0], att.astype(BF16)))
        yield
        pres = []
        for sl, z in zip(cut(j), mixed):
            xh, sc = norm(r.xT[:, sl].astype(F32) + z, 0)
            r.xh1s[:, sl] = xh
            r.r1s[:, sl] = sc
            pres.append(nn(r.tailT[1], (xh * wide_gain(0)).astype(BF16)))
        yield
        branches = []
        for sl, pre in zip(cut(j), pres):
            act, dact = gelu_both(pre)
            actb = act.astype(BF16)
            r.actb[:, sl] = actb
            r.dacts[:, sl] = dact
            branches.append(nn(r.tailT[2], actb))
        yield
        v3s, k3s = [], []
        for sl, y in zip(cut(j), branches):
            xh, sc = norm(r.xh1s[:, sl] * wide_gain(0) + y, 0)
            r.xh2s[:, sl] = xh
            r.r2s[:, sl] = sc
            m2 = (xh * wide_gain(1)).astype(BF16)
            r.m2b[:, sl] = m2
            kv3 = nn(r.w2kvT[...], m2).astype(BF16)
            r.v3T[:, sl] = kv3[D:]
            k3s.append(kv3[0:D])
        yield
        s3 = nn(r.q3B[...], join(k3s))
        yield
        inside = point_lane < lengths[j]
        m = jnp.max(jnp.where(inside, s3, NEG), axis=1, keepdims=True)
        t = jnp.where(inside, s3 - m, NEG)
        r.t3s[:, at] = t
        p = jnp.exp(t)
        full = nt(p.astype(BF16), r.v3T[:, at])
        yield
        r.rden3[j * HS : (j + 1) * HS] = 1.0 / jnp.maximum(jnp.sum(p, axis=1, keepdims=True), 0.5)
        r.num3[j * SP : (j + 1) * SP] = by_head(full.reshape(HEADS, SP, D))
        yield

    g20, g21 = gains[2, 0][None, :], gains[2, 1][None, :]

    def phase4(j):
        hs = slice(j * HS, (j + 1) * HS)
        rden = r.rden3[hs]
        rdx = by_head(jnp.broadcast_to(rden, (HS, D)).reshape(HEADS, SP, D))
        att = r.num3[j * SP : (j + 1) * SP] * rdx
        attb = att.astype(BF16)
        xha, ra = norm(seed8 + nn(attb, r.outw[2]), 1)
        yield
        h1 = xha * g20
        h1b = h1.astype(BF16)
        pre = nn(h1b, r.ff[2, 0])
        yield
        act, dact = gelu_both(pre)
        actb = act.astype(BF16)
        xhb, rb = norm(h1 + nn(actb, r.ff[2, 1]), 1)
        yield
        r.poolrow[j * SEEDS : (j + 1) * SEEDS] = (xhb * g21)[0:SEEDS]
        s = me * spo + j
        cot = jnp.where(s < set_count, r.cot[jnp.minimum(s, set_count - 1)].astype(F32), 0.0)
        d_out = jnp.concatenate([cot, jnp.zeros((SP - SEEDS, D), F32)], axis=0)
        d_b = norm_back(d_out, g21, xhb, rb, 1)
        d_bb = d_b.astype(BF16)
        d_pre = (dact * nt(d_bb, r.ff[2, 1])).astype(BF16)
        yield
        d_h1 = d_b + nt(d_pre, r.ff[2, 0])
        yield
        d_c = norm_back(d_h1, g20, xha, ra, 1)
        d_cb = d_c.astype(BF16)
        d_att = nt(d_cb, r.outw[2])
        yield
        r.d3s[hs] = heads((d_att * rdx).astype(BF16).astype(F32)).astype(BF16)
        r.dd3[hs] = -jnp.sum(heads(d_att * att), axis=1, keepdims=True) * rden
        add("O2", tn(attb, d_cb))
        add("U2", tn(h1b, d_pre))
        add("E2", tn(actb, d_bb))
        add("misc", d_c, DSEED)
        add("misc", jnp.sum(d_h1 * xha, axis=0, keepdims=True), GAIN + 4)
        add("misc", jnp.sum(d_out * xhb, axis=0, keepdims=True), GAIN + 5)
        yield

    def fold(values):
        return total([values[:, k * D : (k + 1) * D] for k in range(values.shape[1] // D)])

    def phase5(j):
        at = lanes(j)
        hs = slice(j * HS, (j + 1) * HS)
        d3 = r.d3s[hs]
        t = r.t3s[:, at]
        p = jnp.exp(t)
        dp = nn(d3, r.v3T[:, at])
        dv3 = tn(d3, p.astype(BF16)).astype(BF16)
        yield
        e = p * (dp + r.dd3[hs])
        ds3 = (e - jnp.where(t == 0.0, jnp.sum(e, axis=1, keepdims=True), 0.0)).astype(BF16)
        d_ms = [
            nn(r.w2d[:, 0:HS], ds3[:, b : b + LB]) + nn(r.w2d[:, D:], dv3[:, b : b + LB]) for b in range(0, rs, LB)
        ]
        yield
        backs, d_bs, folds = [], [], []
        for sl, d_m in zip(cut(j), d_ms):
            xh2 = r.xh2s[:, sl]
            d_b = norm_back(d_m, wide_gain(1), xh2, r.r2s[:, sl], 0)
            folds.append(fold(d_m * xh2))
            d_bs.append(d_b)
            backs.append(nn(r.ff[1, 1], d_b.astype(BF16)))
        r.gacc[1] += total(folds)
        m2 = r.m2b[:, at]
        add("misc", nt(ds3, m2), T3)
        add("W22", nt(m2, dv3))
        yield "W22"
        d_pres = [(r.dacts[:, sl] * back).astype(BF16) for sl, back in zip(cut(j), backs)]
        backs = [nn(r.ff[1, 0], d_pre) for d_pre in d_pres]
        add("E1", nt(r.actb[:, at], join([d_b.astype(BF16) for d_b in d_bs])))
        yield
        d_cbs, d_atts, h1s, folds = [], [], [], []
        for sl, d_b, back in zip(cut(j), d_bs, backs):
            d_h1 = d_b + back
            xh1 = r.xh1s[:, sl]
            d_c = norm_back(d_h1, wide_gain(0), xh1, r.r1s[:, sl], 0)
            r.dxT[:, sl] = d_c
            d_cbs.append(d_c.astype(BF16))
            d_atts.append(nn(r.outw[1], d_cbs[-1]))
            folds.append(fold(d_h1 * xh1))
            h1s.append((xh1 * wide_gain(0)).astype(BF16))
        r.gacc[0] += total(folds)
        add("U1", nt(join(h1s), join(d_pres)))
        yield
        kv2 = r.kv2s[ind_rows(j)]
        kb, vb = blocks(kv2[:, 0:D]), blocks(kv2[:, D:])
        d_nums, dps, ps, ddens, attbs = [], [], [], [], []
        for sl, d_att in zip(cut(j), d_atts):
            att = r.attT[:, sl]
            rden = r.rden2s[:, :, sl]
            d_num = (d_att.reshape(HEADS, HD, LB) * rden).reshape(D, LB).astype(BF16)
            dps.append(nn(vb, d_num))
            ddens.append(-jnp.sum((d_att * att).reshape(HEADS, HD, LB), axis=1, keepdims=True) * rden)
            d_nums.append(d_num)
            attbs.append(att.astype(BF16))
        add("O1", nt(join(attbs), join(d_cbs)))
        yield
        dss, dqs = [], []
        for sl, dp, dden in zip(cut(j), dps, ddens):
            t = r.t2s[:, sl].reshape(HEADS, IND, LB)
            p = jnp.exp(t)
            ps.append(p.reshape(D, LB).astype(BF16))
            e = p * (dp.reshape(HEADS, IND, LB) + dden)
            ds = (e - jnp.where(t == 0.0, jnp.sum(e, axis=1, keepdims=True), 0.0)).reshape(D, LB).astype(BF16)
            dss.append(ds)
            dqs.append(tn(kb, ds))
        dk2 = nt(join(dss), r.q2T[:, at])
        dv2 = nt(join(ps), join(d_nums))
        yield
        dkv2 = join([by_head(dk2.reshape(HEADS, IND, D)), by_head(dv2.reshape(HEADS, IND, D))]).astype(BF16)
        r.dk2s[ind_rows(j)] = nt(dkv2, r.w1kv[...])
        dqbs = []
        for sl, dq in zip(cut(j), dqs):
            dqbs.append((dq * FACTOR).astype(BF16))
            r.dxT[:, sl] += nn(r.proj[1, 0], dqbs[-1])
        dw = tn(r.k2s[ind_rows(j)], dkv2)
        add("W11", dw[:, 0:D])
        add("W12", dw[:, D:])
        add("W10", nt(r.xT[:, at], join(dqbs)))
        yield "W10"

    g00, g01 = gains[0, 0][None, :], gains[0, 1][None, :]

    def phase6(j):
        at = ind_rows(j)
        d_out = r.dk2s[at]
        xha, pre, xhb = r.own0[0, at], r.own0[1, at], r.own0[2, at]
        d_b = norm_back(d_out, g01, xhb, r.own0r[1, at], 1)
        d_bb = d_b.astype(BF16)
        act, dact = gelu_both(pre)
        d_pre = (dact * nt(d_bb, r.ff[0, 1])).astype(BF16)
        yield
        d_h1 = d_b + nt(d_pre, r.ff[0, 0])
        yield
        d_c = norm_back(d_h1, g00, xha, r.own0r[0, at], 1)
        d_cb = d_c.astype(BF16)
        d_att = nt(d_cb, r.outw[0])
        yield
        att = r.att1[at]
        r.dn1[at] = (d_att * r.rdenx[at]).astype(BF16)
        r.dden1[j : j + 1] = -compress(d_att * att) / jnp.maximum(r.den1[j : j + 1], 0.5)
        yield
        add("O0", tn(att.astype(BF16), d_cb))
        add("U0", tn((xha * g00).astype(BF16), d_pre))
        add("E0", tn(act.astype(BF16), d_bb))
        add("misc", d_c, DIND)
        add("misc", jnp.sum(d_h1 * xha, axis=0, keepdims=True), GAIN)
        add("misc", jnp.sum(d_out * xhb, axis=0, keepdims=True), GAIN + 1)
        yield "O0"

    def phase7(j):
        at = lanes(j)
        db = blocks(r.dn1[ind_rows(j)])
        dps = [nt(r.v1s[rows, :], db) for rows in cut(j)]
        yield
        es, dvs = [], []
        for rows, dp in zip(cut(j), dps):
            p = jnp.exp(r.t1s[rows, :])
            es.append(p * (dp + r.dden1[j : j + 1]))
            dvs.append(nn(p.astype(BF16), db).astype(BF16))
        peak = jnp.sum(total(es), axis=0, keepdims=True)
        dss = [(e - jnp.where(r.t1s[rows, :] == 0.0, peak, 0.0)).astype(BF16) for rows, e in zip(cut(j), es)]
        dsdv = join([join(dss, 0), join(dvs, 0)])
        dw = nn(r.xT[:, at], dsdv)
        yield
        add("T", dw[:, 0:D])
        add("W02", dw[:, D:])
        yield "T"
        for k, rows in enumerate(cut(j)):
            grad = nn(dsdv[k * LB : (k + 1) * LB], r.w01T[...]) + r.dxT[:, rows].T
            r.pgs[j, k * LB // WIN : (k + 1) * LB // WIN] = grad.astype(BF16).reshape(LB // WIN, WIN, D)
        r.pgr[j, me] = r.pgs[j, me]
        exchange(("pg", j), "pts", spo + j, lambda dev: r.pgs.at[j, dev], lambda dev: r.pgr.at[j, dev])
        yield

    def slab_refs(k):
        return types.SimpleNamespace(**{x: getattr(r, f"s{k}{x}", None) for x in "bgchrx"})

    def half(ref, which):
        return ref.at[pl.ds(which * groups, groups)]

    def slab_steps(k):
        mats, by_core = SLABS[k]
        u = slab_refs(k)
        rows = slab_rows(len(mats), cfg)
        for (name, _), count in list(marks.items()):
            assert name not in mats or count == spo
        u.b[...] = slabs[k][...].reshape(qn, rows // qn, D).astype(BF16)
        if by_core:
            line, piece = "flat", flat
            exchange(("core", k), "core", k, lambda dev: half(u.b, dev), lambda dev: u.c)
            yield
            arrive(("core", k))
            u.x[...] = (half(u.b, core)[...].astype(F32) + u.c[...].astype(F32)).astype(BF16)
            first, count, base = u.x, groups, core * groups
        else:
            line, piece = "layer", q
            first, count, base = u.b, qn, 0
        exchange(("rs", k), line, k, lambda dev: first.at[dev], lambda dev: u.r.at[dev])
        u.r[piece] = first[piece]
        yield
        arrive(("rs", k))
        u.h[hi] = total([u.r[i].astype(F32) for i in range(count)]).astype(BF16)
        exchange(("z", k), "column", k, lambda dev: u.h.at[hi], lambda dev: u.h.at[dev])
        yield
        arrive(("z", k))
        u.g[base + piece] = total([u.h[i].astype(F32) for i in range(hn)]).astype(BF16)
        exchange(("ag", k), line, len(SLABS) + k, lambda dev: u.g.at[base + piece], lambda dev: u.g.at[base + dev])
        yield
        arrive(("ag", k))
        if by_core:
            exchange(("back", k), "core", len(SLABS) + k, lambda dev: half(u.g, core), lambda dev: half(u.g, dev))
            yield
            arrive(("back", k))

    sums = [slab_steps(k) for k in range(len(SLABS))]

    def step(*which):
        for k in which:
            next(sums[k], None)

    def whole(j):
        for phase in (phase1, phase2, phase3, phase4):
            yield from phase(j)
        if j == spo - 1:
            r.poolall[me] = r.poolrow[...]
            exchange("pool", "pts", 2 * spo, lambda dev: r.poolrow, lambda dev: r.poolall.at[dev])
        for phase in (phase5, phase6, phase7):
            for mark in phase(j):
                if j == spo - 1:
                    if mark == "W22":
                        step(0)
                    elif mark == "W10":
                        for i in range(2):
                            add_gain(i)
                        step(1, 0)
                    elif mark == "O0":
                        step(1)
                    elif mark == "T":
                        step(2)
                yield

    def add_gain(i):
        k, at = WHERE["misc"]
        slabs[k][at + GAIN + 2 + i : at + GAIN + 3 + i] = jnp.sum(r.gacc[i].T, axis=0, keepdims=True)

    streams = [whole(j) for j in range(spo)]
    done = [0] * spo

    def spread(want):
        todo = {j: end - done[j] for j, end in want.items()}
        most = max(todo.values())
        for k in range(1, most + 1):
            for j, count in todo.items():
                while (done[j] - want[j] + count) * most < count * k:
                    next(streams[j], None)
                    done[j] += 1

    if spo == 4:
        for j, want in enumerate(PLAN):
            if j < spo:
                arrive(("x", j))
            spread(want)
    for j in range(spo):
        if spo != 4:
            arrive(("x", j))
    spread({j: STAGES for j in range(spo)})

    sub8 = iota((8, D), 0)

    def unpad(begin, end):
        for t in range(begin, end, 2):
            pieces = []
            for i in (t, t + 1):
                first = r.pgpad[pl.ds(r.first[i], 8), :]
                second = r.pgpad[pl.ds(r.second[i], 8), :]
                pieces.append(jnp.where(sub8 < r.edge[i], first, second))
            r.pg_o[t * 8 : t * 8 + 16, :] = jnp.concatenate(pieces, axis=0).astype(BF16)

    tiles = ROWS // 8
    drain(*[("x", j) for j in range(spo)], ("core", 0), ("core", 1), "pool")
    step(0)
    step(1)
    step(2)
    arrive("pool")
    for s in range(set_count):
        j = s % spo
        r.pool_o[s] = r.poolall[s // spo, j * SEEDS : (j + 1) * SEEDS].astype(BF16)
    drain(("rs", 0), ("rs", 1))
    step(0)
    step(1)
    step(2)
    for j in range(spo):
        arrive(("pg", j))
    for s in range(SLOTS):
        r.pgpad[s * WIN : (s + 1) * WIN, :] = r.pgr[s % spo, s // spo].astype(F32)
    unpad(0, tiles // 2)
    step(0)
    drain(*[("pg", j) for j in range(spo)], ("z", 0), ("z", 1), ("rs", 2))
    unpad(tiles // 2, tiles)
    step(1)

    def mat(name):
        k, at = WHERE[name]
        return slab_refs(k).g[...].reshape(-1, D)[at : at + D]

    def put(name, ref, *at):
        ref[at] = mat(name).astype(F32)

    step(0)
    put("O2", r.outg_o, 2)
    put("U2", r.ffg_o, 2, 0)
    put("E2", r.ffg_o, 2, 1)
    put("W22", r.projg_o, 2, 2)
    drain(("z", 2), ("ag", 0), ("ag", 1), ("back", 0))
    step(1)
    put("O1", r.outg_o, 1)
    put("U1", r.ffg_o, 1, 0)
    put("E1", r.ffg_o, 1, 1)
    for a in range(3):
        put(f"W1{a}", r.projg_o, 1, a)
    step(2)
    tsum = mat("T")
    dq1 = by_head(tn(tsum, r.proj[0, 1]).reshape(HEADS, IND, D)) * FACTOR
    t3 = mat("misc")[T3 : T3 + HS]
    dq3 = by_head(nn(t3, r.proj[2, 1]).reshape(HEADS, SP, D)) * FACTOR
    r.projg_o[0, 1] = nn(tsum, r.qB[...])
    r.projg_o[2, 1] = tn(t3, r.q3B[...])
    misc = mat("misc").astype(F32)
    high, low = split(dq1)
    r.indg_o[...] = misc[DIND : DIND + IND] + nt(high, r.proj[0, 0]) + nt(low, r.proj[0, 0])
    r.projg_o[0, 0] = tn(r.ind[...], high) + tn(r.ind[...], low)
    dq3 = jnp.concatenate([dq3, jnp.zeros((SP, D), F32)], axis=0)
    high, low = split(dq3)
    seed_part = (nt(high, r.proj[2, 0]) + nt(low, r.proj[2, 0]))[0:SEEDS]
    r.seedg_o[...] = seed_part + misc[DSEED : DSEED + SEEDS]
    r.projg_o[2, 0] = tn(seed16, high) + tn(seed16, low)
    for a in range(3):
        r.gaing_o[a] = misc[GAIN + 2 * a : GAIN + 2 * a + 2]
    put("W02", r.projg_o, 0, 2)
    put("O0", r.outg_o, 0)
    put("U0", r.ffg_o, 0, 0)
    put("E0", r.ffg_o, 0, 1)
    flush()


def write_out(*refs):
    n = len(OUT_NAMES)
    sems = refs[2 * n]
    copies = [pltpu.make_async_copy(refs[j], refs[n + j], sems.at[j]) for j in range(n)]
    for c in copies:
        c.start()
    for c in copies:
        c.wait()


def local(parts, groups, points, set_lengths, projections, outputs, feedforward, gains, inducing, seeds, cotangent):
    set_count = set_lengths.shape[0]
    cfg = plan(parts, groups)
    args = (set_lengths, points, projections, outputs, feedforward, gains, inducing, seeds, cotangent)
    table = {}
    for name, a in zip(IN_NAMES, args):
        table[name] = pltpu.SMEM(a.shape, a.dtype) if name == "lens" else pltpu.VMEM(a.shape, a.dtype)
    table.update(scratch_table(cfg))
    vmem = pl.BlockSpec(memory_space=pltpu.VMEM)
    hbm = pl.BlockSpec(memory_space=pltpu.HBM)
    args = tuple(pltpu.with_memory_space_constraint(a, pltpu.HBM) for a in args)
    out_shape = [
        jax.ShapeDtypeStruct((set_count, SEEDS, D), BF16),
        jax.ShapeDtypeStruct(points.shape, BF16),
        jax.ShapeDtypeStruct((3, 3, D, D), F32),
        jax.ShapeDtypeStruct((3, D, D), F32),
        jax.ShapeDtypeStruct((3, 2, D, D), F32),
        jax.ShapeDtypeStruct((3, 2, D), F32),
        jax.ShapeDtypeStruct((IND, D), F32),
        jax.ShapeDtypeStruct((SEEDS, D), F32),
    ]
    n = len(out_shape)
    results = pl.pallas_call(
        functools.partial(kernel, cfg, set_count, tuple(table)),
        out_shape=[pltpu.VMEM(o.shape, o.dtype) for o in out_shape],
        in_specs=[hbm] * len(args),
        out_specs=[vmem] * n,
        scratch_shapes=list(table.values()),
        compiler_params=pltpu.CompilerParams(
            collective_id=0, has_side_effects=True, vmem_limit_bytes=48 * 1024 * 1024
        ),
    )(*args)
    results = [pltpu.with_memory_space_constraint(a, pltpu.VMEM) for a in results]
    return tuple(
        pl.pallas_call(
            write_out,
            out_shape=out_shape,
            in_specs=[vmem] * n,
            out_specs=[hbm] * n,
            scratch_shapes=[pltpu.SemaphoreType.DMA((n,))],
        )(*results)
    )


def solution(mesh):
    parts, groups = mesh.shape["pts"], mesh.shape["sets"]
    placed = (P(("sets", "pts"), None), P("sets"), P(), P(), P(), P(), P(), P(), P("sets", None, None))
    return jax.shard_map(
        functools.partial(local, parts, groups),
        mesh=mesh,
        in_specs=placed,
        out_specs=(P("sets", None, None), P(("sets", "pts"), None), P(), P(), P(), P(), P(), P()),
        check_vma=False,
    )
```
